32 devices in a mesh: dp: 4 (over y, x), expert: 8 (over z, core).
Axes of the slice: x: 2, y: 2, z: 4, core: 2. Of those that a mesh axis runs over, the one named last changes fastest.
Arguments:
- tokens: bfloat16 [4096, 1024], P(('dp', 'expert')), may hold values from -6 to 6
- cotangent: bfloat16 [4096, 1024], P(('dp', 'expert')), may hold values from -6 to 6
- expert_ids: int32 [4096, 8], P(('dp', 'expert')), may hold values from 0 to 15, all different within a row; in each aligned block of 128 rows (0 to 127, 128 to 255, ...) at most 80 rows name the same one
- gate_probs: bfloat16 [4096, 8], P(('dp', 'expert')), may hold values from 0.049804688 to 0.5
- gate_up: bfloat16 [16, 1024, 1024], P('expert', 'dp'), may hold values from -0.1875 to 0.1875
- down_proj: bfloat16 [16, 512, 1024], P('expert', 'dp'), may hold values from -0.25 to 0.25
Outputs:
- grad_tokens: bfloat16 [4096, 1024], P(('dp', 'expert'))
- grad_gates: bfloat16 [4096, 8], P(('dp', 'expert'))
- grad_gate_up: float32 [16, 1024, 1024], P('expert', 'dp')
- grad_down: float32 [16, 512, 1024], P('expert', 'dp')
The draws below stay inside these ranges and needn't reach their ends.
Inputs may be any that keep to these rules, and one draw needn't show every extreme that they name: `expert_ids`: each token names 8 different experts. Among the 128 tokens of one device (aligned blocks of rows) no expert is named more than 80 times, and in every draw some expert is named exactly 80 times by the tokens of some device.
All inputs are finite; a program needn't handle non-finite values.
Results may differ from the reference program's by a relative error of at most 0.0058.
Values may be sent and summed in bfloat16 or wider, within the bound.
A program may use at most 128 MiB of HBM per device.

```python
import math
import jax
import jax.numpy as jnp
import numpy as np
from jax import lax

D = 1024
F = 512
TOP = 8
TOK_DEV = 128
EXPERTS = 16
CAP = 80
TOKENS = 4096


def block_levels(key, dims, split, least, largest):
    gain = 1.0
    for dim, blocks in split:
        steps = jax.random.uniform(jax.random.fold_in(jax.random.fold_in(key, 6), dim), (blocks,), jnp.float32, least / len(split), largest / len(split))
        gain = gain * jnp.repeat(jnp.exp(steps), dims[dim] // blocks).reshape((-1,) + (1,) * (len(dims) - 1 - dim))
    return gain


def assign_block(key, own, number, rows, amount, top, bound, slope):
    ranking = jax.random.permutation(key, amount)
    heavy_load, ordinary = shares(amount, rows * top, bound, slope, True), shares(amount, rows * top, bound, slope, False)
    places = jnp.arange(amount)

    def named(lengths, turn):
        used = int((lengths > 0).sum())
        fixed = max(1, used // 4)
        moved = fixed + (places - fixed + turn * (used - fixed)) % max(1, amount - fixed)
        return jnp.zeros((amount,), jnp.int32).at[ranking[jnp.where(places < fixed, places, moved)]].set(jnp.asarray(lengths, jnp.int32))

    lengths = jnp.where(number % 4 == 0, named(heavy_load, number // 4), named(ordinary, number - number // 4 - 1))
    mixed = jax.random.permutation(jax.random.fold_in(own, 3), amount)
    donor, taker = mixed[0:amount // 2 * 2:2], mixed[1:amount // 2 * 2:2]
    margin = jnp.minimum(lengths[donor] - 1, bound - lengths[taker]) // 2
    margin = jnp.where((donor == ranking[0]) | (taker == ranking[0]) | (lengths[taker] == 0), 0, jnp.maximum(margin, 0))
    moved = jax.random.randint(jax.random.fold_in(own, 4), (amount // 2,), 0, 1 << 20) % (margin + 1)
    lengths = lengths.at[donor].add(-moved).at[taker].add(moved)
    labels = jnp.searchsorted(jnp.cumsum(lengths), jnp.arange(rows * top), side="right").astype(jnp.int32)
    listing = labels.reshape(top, rows).T
    listing = listing[jax.random.permutation(jax.random.fold_in(own, 1), rows)]
    turn = jax.random.randint(jax.random.fold_in(own, 2), (rows, 1), 0, top)
    return jnp.take_along_axis(listing, (jnp.arange(top)[None, :] + turn) % top, axis=1)


def shares(amount, total, limit, lean, full):
    loads = [(1 << 20) // math.isqrt(grade ** lean) + 1 for grade in range(1, amount + 1)]
    largest = limit if full else min(limit, max(-(-total // amount), total * loads[0] // sum(loads)))
    least = 1 if total - largest >= amount - 1 else 0
    given, rest = [largest] + [least] * (amount - 1), total - largest - least * (amount - 1)
    while rest > 0:
        movable = [i for i in range(1, amount) if given[i] < largest] or [i for i in range(1, amount) if given[i] < limit]
        pool, remaining = sum([loads[i] for i in movable]), rest
        for i in movable:
            more = min(limit - given[i], max(1, remaining * loads[i] // pool), rest)
            given[i] = given[i] + more
            rest = rest - more
    return np.array(given)


def noise(key, dims, scale, limit, split=(), held_as=jnp.bfloat16):
    values = jax.random.normal(key, dims, jnp.float32) * scale
    if len(split) > 0:
        values = block_levels(key, dims, split, -0.22, 0.18) * values
    return jnp.clip(values, min=-limit, max=limit).astype(held_as)


def setup_inputs(seed: int = 0) -> dict:
    keys = jax.random.split(jax.random.key(seed), 7)
    tokens = noise(keys[0], (TOKENS, D), 1.0, 6.0, ((0, 32),))
    cotangent = noise(keys[1], (TOKENS, D), 1.0, 6.0, ((0, 32),))
    expert_ids_keys = jax.random.split(jax.random.fold_in(keys[2], 1), TOKENS // TOK_DEV)
    expert_ids_turns = jax.random.permutation(jax.random.fold_in(keys[2], 3), TOKENS // TOK_DEV)
    expert_ids = jax.vmap(lambda own, number: assign_block(jax.random.fold_in(keys[2], 2), own, number, TOK_DEV, EXPERTS, TOP, CAP, 1))(expert_ids_keys, expert_ids_turns).reshape((TOKENS, TOP))
    gate_probs = jnp.clip(0.049804688 + 0.4501953 * jax.random.uniform(keys[3], (TOKENS, TOP), jnp.float32) ** block_levels(keys[3], (TOKENS, TOP), ((0, 32),), -0.2, 0.2), 0.049804688, 0.5).astype(jnp.bfloat16)
    gate_up = noise(keys[4], (EXPERTS, D, 2 * F), D ** -0.5, 0.1875, ((0, 8), (1, 4)))
    down_proj = noise(keys[5], (EXPERTS, F, D), F ** -0.5, 0.25, ((0, 8), (1, 4)))
    return dict(tokens=tokens, cotangent=cotangent, expert_ids=expert_ids, gate_probs=gate_probs, gate_up=gate_up, down_proj=down_proj)


def expert_grads(routed_x, routed_dy, routed_gate, w_in, w_out):
    pre_act = jnp.dot(routed_x, w_in, preferred_element_type=jnp.float32)
    hidden = w_out.shape[0]
    gate_pre = pre_act[:, :hidden]
    up_pre = pre_act[:, hidden:]
    sigmoid_h = jax.nn.sigmoid(gate_pre)
    silu_h = gate_pre * sigmoid_h
    activation = silu_h * up_pre
    raw_grad = jnp.dot(routed_dy, w_out.T, preferred_element_type=jnp.float32)
    gate_col = routed_gate.astype(jnp.float32)[:, None]
    act_grad = gate_col * raw_grad
    grad_gate = act_grad * up_pre * sigmoid_h * (1.0 + gate_pre * (1.0 - sigmoid_h))
    grad_up = act_grad * silu_h
    pre_grad = jnp.concatenate([grad_gate, grad_up], axis=-1).astype(jnp.bfloat16)
    scaled_act = (gate_col * activation).astype(jnp.bfloat16)
    slot_dx = jnp.dot(pre_grad, w_in.T, preferred_element_type=jnp.float32).astype(jnp.bfloat16)
    slot_gate = jnp.sum(activation * raw_grad, axis=-1).astype(jnp.bfloat16)
    return pre_grad, scaled_act, slot_dx, slot_gate


def reference(tokens, cotangent, expert_ids, gate_probs, gate_up, down_proj):
    tok_total, width = tokens.shape
    devices_all = tok_total // TOK_DEV
    per_device = TOK_DEV * TOP
    assign_total = tok_total * TOP
    flat_ids = expert_ids.reshape(devices_all, per_device).astype(jnp.int32)
    onehot = (flat_ids[:, :, None] == jnp.arange(EXPERTS, dtype=jnp.int32)[None, None, :]).astype(jnp.int32)
    before = jnp.cumsum(onehot, axis=1) - onehot
    slot_rank = jnp.sum(before * onehot, axis=2).astype(jnp.int32)
    device_row = jnp.arange(devices_all, dtype=jnp.int32)[:, None]
    column = (device_row * CAP + slot_rank).astype(jnp.int32)
    assigned_all = jnp.arange(assign_total, dtype=jnp.int32).reshape(devices_all, per_device)
    table = jnp.full((EXPERTS, devices_all * CAP), assign_total, jnp.int32).at[flat_ids, column].set(assigned_all)
    flat_gates = gate_probs.reshape(-1)

    def one_expert(carry, inputs):
        grad_acc, gate_acc = carry
        assigned, w_in, w_out = inputs
        valid = assigned < assign_total
        safe_assign = jnp.where(valid, assigned, 0).astype(jnp.int32)
        token_of = (safe_assign // TOP).astype(jnp.int32)
        routed_x = jnp.where(valid[:, None], tokens[token_of], jnp.zeros((), jnp.bfloat16)).astype(jnp.bfloat16)
        routed_dy = jnp.where(valid[:, None], cotangent[token_of], jnp.zeros((), jnp.bfloat16)).astype(jnp.bfloat16)
        routed_gate = jnp.where(valid, flat_gates[safe_assign], jnp.zeros((), jnp.bfloat16)).astype(jnp.bfloat16)
        pre_grad, scaled_act, slot_dx, slot_gate = expert_grads(routed_x, routed_dy, routed_gate, w_in, w_out)
        grad_in = jnp.dot(routed_x.T, pre_grad, preferred_element_type=jnp.float32)
        grad_out = jnp.dot(scaled_act.T, routed_dy, preferred_element_type=jnp.float32)
        target = jnp.where(valid, token_of, tok_total).astype(jnp.int32)
        grad_acc = grad_acc.at[target].add(slot_dx.astype(jnp.float32), mode="drop")
        gate_acc = gate_acc.at[assigned].set(slot_gate.astype(jnp.float32), mode="drop")
        return (grad_acc, gate_acc), (grad_in, grad_out)

    start = (jnp.zeros((tok_total, width), jnp.float32), jnp.zeros((assign_total,), jnp.float32))
    (grad_acc, gate_acc), (grad_gate_up, grad_down) = lax.scan(one_expert, start, (table, gate_up, down_proj))
    grad_tokens = grad_acc.astype(jnp.bfloat16)
    grad_gates = gate_acc.reshape(tok_total, TOP).astype(jnp.bfloat16)
    return grad_tokens, grad_gates, grad_gate_up, grad_down
```

```python
import jax
import jax.numpy as jnp
from jax import lax
from jax.sharding import PartitionSpec as P

EXP_DEV = 2


def body(tokens, cotangent, expert_ids, gate_probs, gate_up, down_proj):
    owners = lax.axis_size("expert")
    experts_all = EXP_DEV * owners
    dp = lax.axis_size("dp")
    rows_in, rows_out = gate_up.shape[1], down_proj.shape[1]
    width, hidden = tokens.shape[1], rows_out * dp
    tok_count = tokens.shape[0]
    chosen = expert_ids[:, :, None] == jnp.arange(experts_all, dtype=jnp.int32)
    dense = jnp.sum(jnp.where(chosen, gate_probs[:, :, None].astype(jnp.float32), 0.0), axis=1)
    dense = dense.astype(jnp.bfloat16)
    all_x = lax.all_gather(tokens, "expert", axis=0, tiled=True)
    all_dy = lax.all_gather(cotangent, "expert", axis=0, tiled=True)
    gates = lax.all_to_all(dense, "expert", split_axis=1, concat_axis=0, tiled=True)
    w_in = lax.all_gather(gate_up, "dp", axis=1, tiled=True)
    w_out = lax.all_gather(down_proj, "dp", axis=1, tiled=True)
    pres, acts, gate_sums = [], [], []
    for j in range(EXP_DEV):
        pre_act = jnp.dot(all_x, w_in[j], preferred_element_type=jnp.float32)
        gate_pre, up_pre = pre_act[:, :hidden], pre_act[:, hidden:]
        sig = jax.nn.sigmoid(gate_pre)
        silu = gate_pre * sig
        act = silu * up_pre
        raw = lax.dot_general(
            all_dy, w_out[j], (((1,), (1,)), ((), ())), preferred_element_type=jnp.float32
        )
        g = gates[:, j : j + 1].astype(jnp.float32)
        act_grad = g * raw
        grad_gate = act_grad * up_pre * sig * (1.0 + gate_pre * (1.0 - sig))
        grad_up = act_grad * silu
        pres.append(jnp.concatenate([grad_gate, grad_up], axis=-1).astype(jnp.bfloat16))
        acts.append((g * act).astype(jnp.bfloat16))
        gate_sums.append(jnp.sum(act * raw, axis=-1, keepdims=True).astype(jnp.bfloat16))

    def scatter(left, right):
        full = lax.dot_general(
            left, right, (((0,), (0,)), ((), ())), preferred_element_type=jnp.float32
        ).astype(jnp.bfloat16)
        return lax.psum_scatter(full, "dp", scatter_dimension=0, tiled=True).astype(jnp.float32)

    grad_gate_up = jnp.stack([scatter(all_x, pres[j]) for j in range(EXP_DEV)])
    grad_down = jnp.stack([scatter(acts[j], all_dy) for j in range(EXP_DEV)])
    dx = sum(
        lax.dot_general(
            pres[j], w_in[j], (((1,), (1,)), ((), ())), preferred_element_type=jnp.float32
        )
        for j in range(EXP_DEV)
    ).astype(jnp.bfloat16)
    grad_tokens = lax.psum_scatter(dx, "expert", scatter_dimension=0, tiled=True)
    back = lax.all_to_all(
        jnp.concatenate(gate_sums, axis=1), "expert", split_axis=0, concat_axis=1, tiled=True
    )
    grad_gates = jnp.sum(
        jnp.where(chosen, back[:, None, :].astype(jnp.float32), 0.0), axis=2
    ).astype(jnp.bfloat16)
    return (grad_tokens, grad_gates, grad_gate_up, grad_down)


def solution(mesh):
    tok = P(("dp", "expert"), None)
    wgt = P("expert", "dp", None)
    return jax.shard_map(
        body,
        mesh=mesh,
        in_specs=(tok, tok, tok, tok, wgt, wgt),
        out_specs=(tok, tok, wgt, wgt),
        check_vma=False,
    )
```

```python
import functools
import math

import jax
import jax.numpy as jnp
from jax import lax
from jax.experimental import pallas as pl
from jax.experimental.pallas import tpu as pltpu
from jax.sharding import PartitionSpec as P

EXP_DEV = 2
LANES = 128
BF16 = jnp.bfloat16
F32 = jnp.float32


def dot(a, b):
    return jnp.dot(a, b, preferred_element_type=F32)


def dot_nt(a, b):
    return lax.dot_general(a, b, (((1,), (1,)), ((), ())), preferred_element_type=F32)


def kernel(
    ny, nx, nz,
    x_ref, dy_ref, ids_ref, gates_ref, wgu_ref, wd_ref,
    gtok_ref, ggate_ref, ggu_ref, gd_ref,
    blocks, x_t, w_in, w_out, pre, act_t, g_in, g_out,
    in_r1a, in_r1b, in_r2a, in_r2b, out_r1a, out_r1b, out_r2a, out_r2b,
    dxp, dx_r1, dx_r2,
    send_sems, recv_sems, up_sems, down_sems, side_sems, chain_sems, pair_sems,
):
    dp, me = lax.axis_index("dp"), lax.axis_index("expert")
    y, x = dp // nx, dp % nx
    z, c = me // 2, me % 2
    tok, width = x_ref.shape
    rows_in, cols_in = wgu_ref.shape[1:]
    rows_out = wd_ref.shape[1]
    half_in, half_out = rows_in // 2, rows_out // 2
    hidden = cols_in // 2
    total = nz * 2 * tok
    top = ids_ref.shape[1]

    def on_y(o):
        return (lax.rem(y + o, ny) * nx + x, me)

    def on_x(o):
        return (y * nx + lax.rem(x + o, nx), me)

    def on_z(zz):
        return (dp, zz * 2 + c)

    partner = (dp, z * 2 + 1 - c)
    peers = [on_y(o) for o in range(1, ny)] + [on_x(o) for o in range(1, nx)]
    peers += [on_z(lax.rem(z + o, nz)) for o in range(1, nz)] + [partner]

    barrier = pltpu.get_barrier_semaphore()
    for peer in peers:
        pl.semaphore_signal(barrier, inc=1, device_id=peer, device_id_type=pl.DeviceIdType.MESH)

    lane = lax.broadcasted_iota(jnp.int32, (tok, LANES), 1)
    dense = jnp.zeros((tok, LANES), F32)
    for k in range(top):
        dense += jnp.where(ids_ref[:, k : k + 1] == lane, gates_ref[:, k : k + 1].astype(F32), 0.0)
    blocks[z, c, :, :width] = x_ref[...]
    blocks[z, c, :, width : 2 * width] = dy_ref[...]
    blocks[z, c, :, 2 * width :] = dense.astype(BF16)
    for j in range(EXP_DEV):
        w_in[j, y, x] = wgu_ref[j].reshape(2, half_in, cols_in)
        w_out[j, y, x] = wd_ref[j].reshape(2, half_out, width)

    pl.semaphore_wait(barrier, len(peers))

    started = []

    def push(src, dst, peer):
        i = len(started)
        copy = pltpu.make_async_remote_copy(
            src_ref=src, dst_ref=dst, send_sem=send_sems.at[i], recv_sem=recv_sems.at[i],
            device_id=peer, device_id_type=pl.DeviceIdType.MESH,
        )
        copy.start()
        started.append(copy)
        return copy

    def arrived(copies):
        for copy in copies:
            copy.wait_recv()

    def block_copy(origin, send_sem, recv_sem, peer):
        ref = blocks.at[origin, c]
        return pltpu.make_async_remote_copy(
            src_ref=ref, dst_ref=ref, send_sem=send_sem, recv_sem=recv_sem,
            device_id=peer, device_id_type=pl.DeviceIdType.MESH,
        )

    def up(origin):
        peer = on_z(jnp.minimum(z + 1, nz - 1))
        return block_copy(origin, up_sems.at[origin], chain_sems.at[origin], peer)

    def down(origin):
        peer = on_z(jnp.maximum(z - 1, 0))
        return block_copy(origin, down_sems.at[origin], chain_sems.at[origin], peer)

    def side(origin):
        return block_copy(origin, side_sems.at[origin], pair_sems.at[origin], partner)

    def transpose(zz, cc):
        at = pl.multiple_of((zz * 2 + cc) * tok, tok)
        x_t[:, pl.ds(at, tok)] = blocks[zz, cc, :, :width].T

    def chain_step(s):
        @pl.when(z - s >= 0)
        def _():
            origin = z - s
            up(origin).wait_recv()

            @pl.when(z < nz - 1)
            def _():
                up(origin).start()

            side(origin).start()
            transpose(origin, c)

        @pl.when(z + s < nz)
        def _():
            origin = z + s
            down(origin).wait_recv()

            @pl.when(z > 0)
            def _():
                down(origin).start()

            side(origin).start()
            transpose(origin, c)

    def weights_first(j):
        copies = []
        for o in range(1, nx):
            for w in (w_in, w_out):
                copies.append(push(w.at[j, y, x, 0], w.at[j, y, x, 0], on_x(o)))
        for o in range(1, ny):
            for w in (w_in, w_out):
                copies.append(push(w.at[j, y, x, 1], w.at[j, y, x, 1], on_y(o)))
        return copies

    def weights_second(j):
        copies = []
        for o in range(1, ny):
            for w in (w_in, w_out):
                copies.append(push(w.at[j, y, :, 0], w.at[j, y, :, 0], on_y(o)))
        for o in range(1, nx):
            for w in (w_in, w_out):
                copies.append(push(w.at[j, :, x, 1], w.at[j, :, x, 1], on_x(o)))
        return copies

    first0 = weights_first(0)

    @pl.when(z < nz - 1)
    def _():
        up(z).start()

    @pl.when(z > 0)
    def _():
        down(z).start()

    side(z).start()
    transpose(z, c)
    arrived(first0)
    second0 = weights_second(0)
    first1 = weights_first(1)
    for s in range(1, nz - 1):
        chain_step(s)
    arrived(first1)
    second1 = weights_second(1)
    chain_step(nz - 1)

    for zz in range(nz):
        side(zz).wait_recv()
        transpose(zz, 1 - c)

    group = min(nz, max(1, 512 // (2 * tok)))
    rows = group * 2 * tok
    glane = lax.broadcasted_iota(jnp.int32, (rows, LANES), 1)

    def forward(j):
        def step(i, carry):
            at = pl.ds(i * group, group)
            gates = blocks[at, :, :, 2 * width :].reshape(rows, LANES).astype(F32)
            mine = glane == EXP_DEV * me + j
            g = jnp.sum(jnp.where(mine, gates, 0.0), axis=1, keepdims=True)
            pre_act = dot(
                blocks[at, :, :, :width].reshape(rows, width), w_in[j].reshape(width, cols_in)
            )
            raw = dot_nt(
                blocks[at, :, :, width : 2 * width].reshape(rows, width),
                w_out[j].reshape(hidden, width),
            )
            gate_pre, up_pre = pre_act[:, :hidden], pre_act[:, hidden:]
            sig = jax.nn.sigmoid(gate_pre)
            silu = gate_pre * sig
            act = silu * up_pre
            act_grad = g * raw
            r = pl.ds(pl.multiple_of(i * rows, rows), rows)
            pre[j, r, :hidden] = (act_grad * up_pre * sig * (1.0 + gate_pre * (1.0 - sig))).astype(BF16)
            pre[j, r, hidden:] = (act_grad * silu).astype(BF16)
            act_t[:, r] = (g * act).astype(BF16).T
            sums = jnp.sum(act * raw, axis=1, keepdims=True)
            placed = jnp.where(mine, sums, 0.0)
            if j > 0:
                placed += dxp[at, :, :, width:].reshape(rows, LANES).astype(F32)
            dxp[at, :, :, width:] = placed.astype(BF16).reshape(group, 2, tok, LANES)
            return carry

        lax.fori_loop(0, nz // group, step, 0)

    def gradients(j):
        def step(yy, carry):
            r_in, r_out = nx * rows_in, nx * rows_out
            part = dot(x_t[pl.ds(pl.multiple_of(yy * r_in, r_in), r_in), :], pre[j])
            g_in[j, yy] = part.astype(BF16).reshape(nx, 2, half_in, cols_in)
            part = dot(
                act_t[pl.ds(pl.multiple_of(yy * r_out, r_out), r_out), :],
                blocks[:, :, :, width : 2 * width].reshape(total, width),
            )
            g_out[j, yy] = part.astype(BF16).reshape(nx, 2, half_out, width)
            return carry

        lax.fori_loop(0, ny, step, 0)

    kinds = (
        (g_in, in_r1a, in_r1b, in_r2a, in_r2b, ggu_ref, half_in),
        (g_out, out_r1a, out_r1b, out_r2a, out_r2b, gd_ref, half_out),
    )

    def sums_first(j):
        copies = []
        for grad, r1a, r1b, _, _, _, _ in kinds:
            for o in range(1, ny):
                to = lax.rem(y + o, ny)
                copies.append(push(grad.at[j, to, :, 0], r1a.at[j, o - 1], on_y(o)))
            for o in range(1, nx):
                to = lax.rem(x + o, nx)
                copies.append(push(grad.at[j, :, to, 1], r1b.at[j, o - 1], on_x(o)))
        return copies

    def sums_second(j):
        copies = []
        for grad, r1a, r1b, r2a, r2b, out, half in kinds:
            for o in range(nx):
                to = lax.rem(x + o, nx)
                value = grad[j, y, to, 0].astype(F32)
                for n in range(ny - 1):
                    value += r1a[j, n, to].astype(F32)
                if o == 0:
                    out[j, :half] = value
                else:
                    grad[j, y, to, 0] = value.astype(BF16)
                    copies.append(push(grad.at[j, y, to, 0], r2a.at[j, o - 1], on_x(o)))
            for o in range(ny):
                to = lax.rem(y + o, ny)
                value = grad[j, to, x, 1].astype(F32)
                for n in range(nx - 1):
                    value += r1b[j, n, to].astype(F32)
                if o == 0:
                    out[j, half:] = value
                else:
                    grad[j, to, x, 1] = value.astype(BF16)
                    copies.append(push(grad.at[j, to, x, 1], r2b.at[j, o - 1], on_y(o)))
        return copies

    def sums_last(j):
        for _, _, _, r2a, r2b, out, half in kinds:
            value = out[j, :half]
            for n in range(nx - 1):
                value += r2a[j, n].astype(F32)
            out[j, :half] = value
            value = out[j, half:]
            for n in range(ny - 1):
                value += r2b[j, n].astype(F32)
            out[j, half:] = value

    arrived(second0)
    forward(0)
    gradients(0)
    sums0 = sums_first(0)
    arrived(second1)
    forward(1)
    gradients(1)
    arrived(sums0)
    last0 = sums_second(0)
    sums1 = sums_first(1)

    def dx_step(i, carry):
        r = pl.ds(pl.multiple_of(i * rows, rows), rows)
        value = dot_nt(pre[0, r, :], w_in[0].reshape(width, cols_in))
        value += dot_nt(pre[1, r, :], w_in[1].reshape(width, cols_in))
        at = pl.ds(i * group, group)
        dxp[at, :, :, :width] = value.astype(BF16).reshape(group, 2, tok, width)
        return carry

    lax.fori_loop(0, nz // group, dx_step, 0)
    pair = push(dxp.at[:, 1 - c], dx_r1, partner)
    arrived([pair])
    spread = []
    for o in range(1, nz):
        to = lax.rem(z + o, nz)
        dxp[to, c] = (dxp[to, c].astype(F32) + dx_r1[to].astype(F32)).astype(BF16)
        spread.append(push(dxp.at[to, c], dx_r2.at[o - 1], on_z(to)))

    arrived(last0)
    sums_last(0)
    arrived(sums1)
    last1 = sums_second(1)

    arrived(spread)
    value = dxp[z, c].astype(F32) + dx_r1[z].astype(F32)
    for n in range(nz - 1):
        value += dx_r2[n].astype(F32)
    gtok_ref[...] = value[:, :width].astype(BF16)
    back = value[:, width:]
    picked = jnp.zeros((tok, LANES), F32)
    for k in range(top):
        one = jnp.sum(jnp.where(ids_ref[:, k : k + 1] == lane, back, 0.0), axis=1, keepdims=True)
        picked += jnp.where(lane == k, one, 0.0)
    ggate_ref[...] = picked[:, :top].astype(BF16)

    arrived(last1)
    sums_last(1)

    for copy in started:
        copy.wait_send()

    def drain(origin):
        side(origin).wait_send()

        @pl.when((origin <= z) & (z < nz - 1))
        def _():
            up(origin).wait_send()

        @pl.when((origin >= z) & (z > 0))
        def _():
            down(origin).wait_send()

    for zz in range(nz):
        drain(zz)


def body(ny, nx, nz, tokens, cotangent, expert_ids, gate_probs, gate_up, down_proj):
    tok, width = tokens.shape
    rows_in, cols_in = gate_up.shape[1:]
    rows_out = down_proj.shape[1]
    hi, ho = rows_in // 2, rows_out // 2
    total = nz * 2 * tok
    copies = 16 * (nx + ny - 2) + nz
    V = pltpu.VMEM
    dma = pltpu.SemaphoreType.DMA
    e = EXP_DEV
    flops = 2 * e * total * width * cols_in * 4
    return pl.pallas_call(
        functools.partial(kernel, ny, nx, nz),
        out_shape=(
            jax.ShapeDtypeStruct(tokens.shape, BF16),
            jax.ShapeDtypeStruct(gate_probs.shape, BF16),
            jax.ShapeDtypeStruct(gate_up.shape, F32),
            jax.ShapeDtypeStruct(down_proj.shape, F32),
        ),
        in_specs=[pl.BlockSpec(memory_space=V)] * 6,
        out_specs=[pl.BlockSpec(memory_space=V)] * 4,
        scratch_shapes=[
            V((nz, 2, tok, 2 * width + LANES), BF16),
            V((width, total), BF16),
            V((e, ny, nx, 2, hi, cols_in), BF16),
            V((e, ny, nx, 2, ho, width), BF16),
            V((e, total, cols_in), BF16),
            V((cols_in // 2, total), BF16),
            V((e, ny, nx, 2, hi, cols_in), BF16),
            V((e, ny, nx, 2, ho, width), BF16),
            V((e, ny - 1, nx, hi, cols_in), BF16),
            V((e, nx - 1, ny, hi, cols_in), BF16),
            V((e, nx - 1, hi, cols_in), BF16),
            V((e, ny - 1, hi, cols_in), BF16),
            V((e, ny - 1, nx, ho, width), BF16),
            V((e, nx - 1, ny, ho, width), BF16),
            V((e, nx - 1, ho, width), BF16),
            V((e, ny - 1, ho, width), BF16),
            V((nz, 2, tok, width + LANES), BF16),
            V((nz, tok, width + LANES), BF16),
            V((nz - 1, tok, width + LANES), BF16),
            dma((copies,)),
            dma((copies,)),
            dma((nz,)),
            dma((nz,)),
            dma((nz,)),
            dma((nz,)),
            dma((nz,)),
        ],
        compiler_params=pltpu.CompilerParams(
            collective_id=0, has_side_effects=True, vmem_limit_bytes=60 * 2**20
        ),
        cost_estimate=pl.CostEstimate(flops=flops, bytes_accessed=8 * 2**20, transcendentals=0),
    )(tokens, cotangent, expert_ids, gate_probs, gate_up, down_proj)


def solution(mesh):
    dp = mesh.shape["dp"]
    nx = next(n for n in range(math.isqrt(dp), 0, -1) if dp % n == 0)
    tok = P(("dp", "expert"), None)
    wgt = P("expert", "dp", None)
    return jax.shard_map(
        functools.partial(body, dp // nx, nx, mesh.shape["expert"] // 2),
        mesh=mesh,
        in_specs=(tok, tok, tok, tok, wgt, wgt),
        out_specs=(tok, tok, wgt, wgt),
        check_vma=False,
    )
```

```python
import functools
import math

import jax
import jax.numpy as jnp
from jax import lax
from jax.experimental import pallas as pl
from jax.experimental.pallas import tpu as pltpu
from jax.sharding import PartitionSpec as P

EXP_DEV = 2
LANES = 128
BF16 = jnp.bfloat16
F32 = jnp.float32


def dot(a, b):
    return jnp.dot(a, b, preferred_element_type=F32)


def dot_nt(a, b):
    return lax.dot_general(a, b, (((1,), (1,)), ((), ())), preferred_element_type=F32)


def kernel(
    ny, nx, nz,
    x_ref, dy_ref, ids_ref, gates_ref, wgu_ref, wd_ref,
    gtok_ref, ggate_ref, ggu_ref, gd_ref,
    blocks, x_t, w_in, w_out, pre, act_t, g_in, g_out,
    in_r1a, in_r1b, in_r2a, in_r2b, out_r1a, out_r1b, out_r2a, out_r2b,
    dxp, dx_r1, dx_r2,
    send_sems, recv_sems, up_sems, down_sems, side_sems, chain_sems, pair_sems, own_sems,
):
    dp, me = lax.axis_index("dp"), lax.axis_index("expert")
    y, x = dp // nx, dp % nx
    z, c = me // 2, me % 2
    tok, width = x_ref.shape
    half_in, cols_in = wgu_ref.shape[2:]
    half_out = wd_ref.shape[2]
    rows_in, rows_out = 2 * half_in, 2 * half_out
    hidden = cols_in // 2
    total = nz * 2 * tok
    top = ids_ref.shape[0]

    def on_y(o):
        return (lax.rem(y + o, ny) * nx + x, me)

    def on_x(o):
        return (y * nx + lax.rem(x + o, nx), me)

    def on_z(zz):
        return (dp, zz * 2 + c)

    partner = (dp, z * 2 + 1 - c)
    peers = [on_y(o) for o in range(1, ny)] + [on_x(o) for o in range(1, nx)]
    peers += [on_z(lax.rem(z + o, nz)) for o in range(1, nz)] + [partner]

    barrier = pltpu.get_barrier_semaphore()
    for peer in peers:
        pl.semaphore_signal(barrier, inc=1, device_id=peer, device_id_type=pl.DeviceIdType.MESH)

    own = []
    for j in range(EXP_DEV):
        own.append(pltpu.make_async_copy(wgu_ref.at[j], w_in.at[j, y, x], own_sems.at[2 * j]))
        own.append(pltpu.make_async_copy(wd_ref.at[j], w_out.at[j, y, x], own_sems.at[2 * j + 1]))
    for copy in own:
        copy.start()

    expert = lax.broadcasted_iota(jnp.int32, (LANES, tok), 0)
    ids = ids_ref[...]
    gate_rows = gates_ref[...].astype(F32)
    dense = jnp.zeros((LANES, tok), F32)
    for k in range(top):
        dense += jnp.where(ids[k : k + 1] == expert, gate_rows[k : k + 1], 0.0)
    blocks[z, c, :, :width] = x_ref[...]
    blocks[z, c, :, width : 2 * width] = dy_ref[...]
    blocks[z, c, :, 2 * width :] = dense.T.astype(BF16)

    pl.semaphore_wait(barrier, len(peers))

    started = []

    def push(src, dst, peer):
        i = len(started)
        copy = pltpu.make_async_remote_copy(
            src_ref=src, dst_ref=dst, send_sem=send_sems.at[i], recv_sem=recv_sems.at[i],
            device_id=peer, device_id_type=pl.DeviceIdType.MESH,
        )
        copy.start()
        started.append(copy)
        return copy

    def arrived(copies):
        for copy in copies:
            copy.wait_recv()

    def block_copy(origin, send_sem, recv_sem, peer):
        ref = blocks.at[origin, c]
        return pltpu.make_async_remote_copy(
            src_ref=ref, dst_ref=ref, send_sem=send_sem, recv_sem=recv_sem,
            device_id=peer, device_id_type=pl.DeviceIdType.MESH,
        )

    def up(origin):
        peer = on_z(jnp.minimum(z + 1, nz - 1))
        return block_copy(origin, up_sems.at[origin], chain_sems.at[origin], peer)

    def down(origin):
        peer = on_z(jnp.maximum(z - 1, 0))
        return block_copy(origin, down_sems.at[origin], chain_sems.at[origin], peer)

    def side(origin):
        return block_copy(origin, side_sems.at[origin], pair_sems.at[origin], partner)

    def transpose(zz, cc):
        at = pl.multiple_of((zz * 2 + cc) * tok, tok)
        x_t[:, pl.ds(at, tok)] = blocks[zz, cc, :, :width].T

    def chain_step(s):
        @pl.when(z - s >= 0)
        def _():
            origin = z - s
            up(origin).wait_recv()

            @pl.when(z < nz - 1)
            def _():
                up(origin).start()

            side(origin).start()
            transpose(origin, c)

        @pl.when(z + s < nz)
        def _():
            origin = z + s
            down(origin).wait_recv()

            @pl.when(z > 0)
            def _():
                down(origin).start()

            side(origin).start()
            transpose(origin, c)

    def weights_first(j):
        copies = []
        for o in range(1, nx):
            for ref, w in ((wgu_ref, w_in), (wd_ref, w_out)):
                copies.append(push(ref.at[j, 0], w.at[j, y, x, 0], on_x(o)))
        for o in range(1, ny):
            for ref, w in ((wgu_ref, w_in), (wd_ref, w_out)):
                copies.append(push(ref.at[j, 1], w.at[j, y, x, 1], on_y(o)))
        return copies

    def weights_second(j):
        copies = []
        for o in range(1, ny):
            for w in (w_in, w_out):
                copies.append(push(w.at[j, y, :, 0], w.at[j, y, :, 0], on_y(o)))
        for o in range(1, nx):
            for w in (w_in, w_out):
                copies.append(push(w.at[j, :, x, 1], w.at[j, :, x, 1], on_x(o)))
        return copies

    first0 = weights_first(0)

    @pl.when(z < nz - 1)
    def _():
        up(z).start()

    @pl.when(z > 0)
    def _():
        down(z).start()

    side(z).start()
    transpose(z, c)
    for copy in own:
        copy.wait()
    arrived(first0)
    second0 = weights_second(0)
    first1 = weights_first(1)

    def forward(j, first, group):
        rows = group * 2 * tok
        glane = lax.broadcasted_iota(jnp.int32, (rows, LANES), 1)
        at = pl.ds(first, group)
        gates = blocks[at, :, :, 2 * width :].reshape(rows, LANES).astype(F32)
        mine = glane == EXP_DEV * me + j
        g = jnp.sum(jnp.where(mine, gates, 0.0), axis=1, keepdims=True)
        pre_act = dot(
            blocks[at, :, :, :width].reshape(rows, width), w_in[j].reshape(width, cols_in)
        )
        raw = dot_nt(
            blocks[at, :, :, width : 2 * width].reshape(rows, width),
            w_out[j].reshape(hidden, width),
        )
        gate_pre, up_pre = pre_act[:, :hidden], pre_act[:, hidden:]
        sig = jax.nn.sigmoid(gate_pre)
        silu = gate_pre * sig
        act = silu * up_pre
        act_grad = g * raw
        r = pl.ds(pl.multiple_of(first * (2 * tok), 2 * tok), rows)
        pre[j, r, :hidden] = (act_grad * up_pre * sig * (1.0 + gate_pre * (1.0 - sig))).astype(BF16)
        pre[j, r, hidden:] = (act_grad * silu).astype(BF16)
        act_t[:, r] = (g * act).astype(BF16).T
        sums = jnp.sum(act * raw, axis=1, keepdims=True)
        placed = jnp.where(mine, sums, 0.0)
        if j > 0:
            placed += dxp[at, :, :, width:].reshape(rows, LANES).astype(F32)
        dxp[at, :, :, width:] = placed.astype(BF16).reshape(group, 2, tok, LANES)

    near = jnp.minimum(z, nz - 1 - z)

    def by_distance(n):
        s = (n + 1) // 2
        close = jnp.where(n % 2 == 1, z - s, z + s)
        far = jnp.where(z == near, n, nz - 1 - n)
        return jnp.where(n <= 2 * near, close, far)

    def forward_arrived(n, carry):
        origin = by_distance(n)
        side(origin).wait_recv()
        transpose(origin, 1 - c)
        forward(0, origin, 1)
        return carry

    group = min(nz, max(1, 512 // (2 * tok)))
    rows = group * 2 * tok

    def forward_all(i, carry):
        forward(1, i * group, group)
        return carry

    def gradients_in(j):
        def step(yy, carry):
            r_in = nx * rows_in
            part = dot(x_t[pl.ds(pl.multiple_of(yy * r_in, r_in), r_in), :], pre[j])
            g_in[j, yy] = part.astype(BF16).reshape(nx, 2, half_in, cols_in)
            return carry

        lax.fori_loop(0, ny, step, 0)

    def gradients_out(j):
        def step(yy, carry):
            r_out = nx * rows_out
            part = dot(
                act_t[pl.ds(pl.multiple_of(yy * r_out, r_out), r_out), :],
                blocks[:, :, :, width : 2 * width].reshape(total, width),
            )
            g_out[j, yy] = part.astype(BF16).reshape(nx, 2, half_out, width)
            return carry

        lax.fori_loop(0, ny, step, 0)

    kinds = (
        (g_in, in_r1a, in_r1b, in_r2a, in_r2b, ggu_ref, half_in),
        (g_out, out_r1a, out_r1b, out_r2a, out_r2b, gd_ref, half_out),
    )

    def sums_first(j, kind):
        grad, r1a, r1b = kind[:3]
        along_y, along_x = [], []
        for o in range(1, ny):
            to = lax.rem(y + o, ny)
            along_y.append(push(grad.at[j, to, :, 0], r1a.at[j, o - 1], on_y(o)))
        for o in range(1, nx):
            to = lax.rem(x + o, nx)
            along_x.append(push(grad.at[j, :, to, 1], r1b.at[j, o - 1], on_x(o)))
        return along_y, along_x

    def sums_second(j, kind, firsts):
        grad, r1a, r1b, r2a, r2b, out, half = kind
        along_x, along_y = [], []
        arrived(firsts[0])
        for o in reversed(range(nx)):
            to = lax.rem(x + o, nx)
            value = grad[j, y, to, 0].astype(F32)
            for n in range(ny - 1):
                value += r1a[j, n, to].astype(F32)
            if o == 0:
                out[j, :half] = value
            else:
                grad[j, y, to, 0] = value.astype(BF16)
                along_x.append(push(grad.at[j, y, to, 0], r2a.at[j, o - 1], on_x(o)))
        arrived(firsts[1])
        for o in reversed(range(ny)):
            to = lax.rem(y + o, ny)
            value = grad[j, to, x, 1].astype(F32)
            for n in range(nx - 1):
                value += r1b[j, n, to].astype(F32)
            if o == 0:
                out[j, half:] = value
            else:
                grad[j, to, x, 1] = value.astype(BF16)
                along_y.append(push(grad.at[j, to, x, 1], r2b.at[j, o - 1], on_y(o)))
        return along_x, along_y

    def sums_last(j, kind, seconds):
        r2a, r2b, out, half = kind[3:]
        arrived(seconds[0])
        value = out[j, :half]
        for n in range(nx - 1):
            value += r2a[j, n].astype(F32)
        out[j, :half] = value
        arrived(seconds[1])
        value = out[j, half:]
        for n in range(ny - 1):
            value += r2b[j, n].astype(F32)
        out[j, half:] = value

    for s in range(1, nz - 1):
        chain_step(s)
    arrived(second0)
    lax.fori_loop(0, nz - 1, forward_arrived, 0)
    arrived(first1)
    second1 = weights_second(1)
    chain_step(nz - 1)
    forward_arrived(nz - 1, 0)
    gradients_in(0)
    firsts0 = [sums_first(0, kinds[0])]
    gradients_out(0)
    firsts0.append(sums_first(0, kinds[1]))
    arrived(second1)
    lax.fori_loop(0, nz // group, forward_all, 0)
    gradients_in(1)
    firsts1 = [sums_first(1, kinds[0])]
    gradients_out(1)
    firsts1.append(sums_first(1, kinds[1]))

    def dx_step(i, carry):
        r = pl.ds(pl.multiple_of(i * rows, rows), rows)
        value = dot_nt(pre[0, r, :], w_in[0].reshape(width, cols_in))
        value += dot_nt(pre[1, r, :], w_in[1].reshape(width, cols_in))
        at = pl.ds(i * group, group)
        dxp[at, :, :, :width] = value.astype(BF16).reshape(group, 2, tok, width)
        return carry

    lax.fori_loop(0, nz // group, dx_step, 0)
    pair = push(dxp.at[:, 1 - c], dx_r1, partner)
    seconds0 = [sums_second(0, kind, first) for kind, first in zip(kinds, firsts0)]
    arrived([pair])
    spread = []
    for o in range(1, nz):
        to = lax.rem(z + o, nz)
        dxp[to, c] = (dxp[to, c].astype(F32) + dx_r1[to].astype(F32)).astype(BF16)
        spread.append(push(dxp.at[to, c], dx_r2.at[o - 1], on_z(to)))

    seconds1 = [sums_second(1, kind, first) for kind, first in zip(kinds, firsts1)]
    for kind, second in zip(kinds, seconds0):
        sums_last(0, kind, second)

    arrived(spread)
    value = dxp[z, c].astype(F32) + dx_r1[z].astype(F32)
    for n in range(nz - 1):
        value += dx_r2[n].astype(F32)
    gtok_ref[...] = value[:, :width].astype(BF16)
    back = value[:, width:].T
    for k in range(top):
        ggate_ref[k : k + 1, :] = jnp.sum(
            jnp.where(ids[k : k + 1] == expert, back, 0.0), axis=0, keepdims=True
        )

    for kind, second in zip(kinds, seconds1):
        sums_last(1, kind, second)

    for copy in started:
        copy.wait_send()

    def drain(origin):
        side(origin).wait_send()

        @pl.when((origin <= z) & (z < nz - 1))
        def _():
            up(origin).wait_send()

        @pl.when((origin >= z) & (z > 0))
        def _():
            down(origin).wait_send()

    for zz in range(nz):
        drain(zz)


def emit(gtok, ggu, gd, gtok_out, ggu_out, gd_out, sems):
    copies = [(gtok, gtok_out)]
    for j in range(EXP_DEV):
        for src, dst in ((ggu, ggu_out), (gd, gd_out)):
            half = src.shape[1] // 2
            for h in range(2):
                at = pl.ds(h * half, half)
                copies.append((src.at[j, at], dst.at[j, at]))
    copies = [pltpu.make_async_copy(s, d, sems.at[i]) for i, (s, d) in enumerate(copies)]
    for copy in copies:
        copy.start()
    for copy in copies:
        copy.wait()


def body(ny, nx, nz, tokens, cotangent, expert_ids, gate_probs, gate_up, down_proj):
    tok, width = tokens.shape
    rows_in, cols_in = gate_up.shape[1:]
    rows_out = down_proj.shape[1]
    hi, ho = rows_in // 2, rows_out // 2
    total = nz * 2 * tok
    copies = 16 * (nx + ny - 2) + nz
    V = pltpu.VMEM
    dma = pltpu.SemaphoreType.DMA
    e = EXP_DEV
    flops = 2 * e * total * width * cols_in * 4
    gtok, ggate, ggu, gd = pl.pallas_call(
        functools.partial(kernel, ny, nx, nz),
        out_shape=(
            jax.ShapeDtypeStruct(tokens.shape, BF16),
            jax.ShapeDtypeStruct(gate_probs.shape[::-1], F32),
            jax.ShapeDtypeStruct(gate_up.shape, F32),
            jax.ShapeDtypeStruct(down_proj.shape, F32),
        ),
        in_specs=[pl.BlockSpec(memory_space=V)] * 4 + [pl.BlockSpec(memory_space=pl.ANY)] * 2,
        out_specs=[pl.BlockSpec(memory_space=V)] * 4,
        scratch_shapes=[
            V((nz, 2, tok, 2 * width + LANES), BF16),
            V((width, total), BF16),
            V((e, ny, nx, 2, hi, cols_in), BF16),
            V((e, ny, nx, 2, ho, width), BF16),
            V((e, total, cols_in), BF16),
            V((cols_in // 2, total), BF16),
            V((e, ny, nx, 2, hi, cols_in), BF16),
            V((e, ny, nx, 2, ho, width), BF16),
            V((e, ny - 1, nx, hi, cols_in), BF16),
            V((e, nx - 1, ny, hi, cols_in), BF16),
            V((e, nx - 1, hi, cols_in), BF16),
            V((e, ny - 1, hi, cols_in), BF16),
            V((e, ny - 1, nx, ho, width), BF16),
            V((e, nx - 1, ny, ho, width), BF16),
            V((e, nx - 1, ho, width), BF16),
            V((e, ny - 1, ho, width), BF16),
            V((nz, 2, tok, width + LANES), BF16),
            V((nz, tok, width + LANES), BF16),
            V((nz - 1, tok, width + LANES), BF16),
            dma((copies,)),
            dma((copies,)),
            dma((nz,)),
            dma((nz,)),
            dma((nz,)),
            dma((nz,)),
            dma((nz,)),
            dma((4,)),
        ],
        compiler_params=pltpu.CompilerParams(
            collective_id=0, has_side_effects=True, vmem_limit_bytes=60 * 2**20
        ),
        cost_estimate=pl.CostEstimate(flops=flops, bytes_accessed=8 * 2**20, transcendentals=0),
    )(
        tokens, cotangent, expert_ids.T, gate_probs.T,
        gate_up.reshape(e, 2, hi, cols_in), down_proj.reshape(e, 2, ho, width),
    )
    gtok, ggu, gd = pl.pallas_call(
        emit,
        out_shape=tuple(jax.ShapeDtypeStruct(a.shape, a.dtype) for a in (gtok, ggu, gd)),
        in_specs=[pl.BlockSpec(memory_space=pl.ANY)] * 3,
        out_specs=[pl.BlockSpec(memory_space=pl.ANY)] * 3,
        scratch_shapes=[dma((4 * e + 1,))],
        compiler_params=pltpu.CompilerParams(vmem_limit_bytes=60 * 2**20),
    )(gtok, ggu, gd)
    return gtok, ggate.astype(BF16).T, ggu, gd


def solution(mesh):
    dp = mesh.shape["dp"]
    nx = next(n for n in range(math.isqrt(dp), 0, -1) if dp % n == 0)
    tok = P(("dp", "expert"), None)
    wgt = P("expert", "dp", None)
    return jax.shard_map(
        functools.partial(body, dp // nx, nx, mesh.shape["expert"] // 2),
        mesh=mesh,
        in_specs=(tok, tok, tok, tok, wgt, wgt),
        out_specs=(tok, tok, wgt, wgt),
        check_vma=False,
    )
```

```python
import functools
import math

import jax
import jax.numpy as jnp
from jax import lax
from jax.experimental import pallas as pl
from jax.experimental.pallas import tpu as pltpu
from jax.sharding import PartitionSpec as P

EXP_DEV = 2
LANES = 128
BF16 = jnp.bfloat16
F32 = jnp.float32


def dot(a, b):
    return jnp.dot(a, b, preferred_element_type=F32)


def dot_nt(a, b):
    return lax.dot_general(a, b, (((1,), (1,)), ((), ())), preferred_element_type=F32)


def kernel(
    ny, nx, nz,
    x_ref, dy_ref, ids_ref, gates_ref, wgu_ref, wd_ref,
    gtok_ref, ggate_ref, ggu_ref, gd_ref,
    blocks, x_t, w_in, w_out, pre, act_t, g_in, g_out,
    in_r1a, in_r1b, in_r2a, in_r2b, out_r1a, out_r1b, out_r2a, out_r2b,
    dxp, dx_r1, dx_r2,
    send_sems, recv_sems, up_sems, down_sems, side_sems, chain_sems, pair_sems, own_sems,
    dxp_send, dxp_recv, dxs_send, dxs_recv,
):
    dp, me = lax.axis_index("dp"), lax.axis_index("expert")
    y, x = dp // nx, dp % nx
    z, c = me // 2, me % 2
    tok, width = x_ref.shape
    half_in, cols_in = wgu_ref.shape[2:]
    half_out = wd_ref.shape[2]
    rows_in, rows_out = 2 * half_in, 2 * half_out
    hidden = cols_in // 2
    total = nz * 2 * tok
    top = ids_ref.shape[0]

    def on_y(o):
        return (lax.rem(y + o, ny) * nx + x, me)

    def on_x(o):
        return (y * nx + lax.rem(x + o, nx), me)

    def on_z(zz):
        return (dp, zz * 2 + c)

    partner = (dp, z * 2 + 1 - c)
    peers = [on_y(o) for o in range(1, ny)] + [on_x(o) for o in range(1, nx)]
    peers += [on_z(lax.rem(z + o, nz)) for o in range(1, nz)] + [partner]

    barrier = pltpu.get_barrier_semaphore()
    for peer in peers:
        pl.semaphore_signal(barrier, inc=1, device_id=peer, device_id_type=pl.DeviceIdType.MESH)

    own = []
    for j in range(EXP_DEV):
        own.append(pltpu.make_async_copy(wgu_ref.at[j], w_in.at[j, y, x], own_sems.at[2 * j]))
        own.append(pltpu.make_async_copy(wd_ref.at[j], w_out.at[j, y, x], own_sems.at[2 * j + 1]))
    for copy in own:
        copy.start()

    expert = lax.broadcasted_iota(jnp.int32, (LANES, tok), 0)
    ids = ids_ref[...]
    gate_rows = gates_ref[...].astype(F32)
    dense = jnp.zeros((LANES, tok), F32)
    for k in range(top):
        dense += jnp.where(ids[k : k + 1] == expert, gate_rows[k : k + 1], 0.0)
    blocks[z, c, :, :width] = x_ref[...]
    blocks[z, c, :, width : 2 * width] = dy_ref[...]
    blocks[z, c, :, 2 * width :] = dense.T.astype(BF16)

    pl.semaphore_wait(barrier, len(peers))

    started = []

    def push(src, dst, peer):
        i = len(started)
        copy = pltpu.make_async_remote_copy(
            src_ref=src, dst_ref=dst, send_sem=send_sems.at[i], recv_sem=recv_sems.at[i],
            device_id=peer, device_id_type=pl.DeviceIdType.MESH,
        )
        copy.start()
        started.append(copy)
        return copy

    def arrived(copies):
        for copy in copies:
            copy.wait_recv()

    def block_copy(origin, send_sem, recv_sem, peer):
        ref = blocks.at[origin, c]
        return pltpu.make_async_remote_copy(
            src_ref=ref, dst_ref=ref, send_sem=send_sem, recv_sem=recv_sem,
            device_id=peer, device_id_type=pl.DeviceIdType.MESH,
        )

    def up(origin):
        peer = on_z(jnp.minimum(z + 1, nz - 1))
        return block_copy(origin, up_sems.at[origin], chain_sems.at[origin], peer)

    def down(origin):
        peer = on_z(jnp.maximum(z - 1, 0))
        return block_copy(origin, down_sems.at[origin], chain_sems.at[origin], peer)

    def side(origin):
        return block_copy(origin, side_sems.at[origin], pair_sems.at[origin], partner)

    def transpose(zz, cc):
        at = pl.multiple_of((zz * 2 + cc) * tok, tok)
        x_t[:, pl.ds(at, tok)] = blocks[zz, cc, :, :width].T

    def chain_step(s):
        @pl.when(z - s >= 0)
        def _():
            origin = z - s
            up(origin).wait_recv()

            @pl.when(z < nz - 1)
            def _():
                up(origin).start()

            side(origin).start()
            transpose(origin, c)

        @pl.when(z + s < nz)
        def _():
            origin = z + s
            down(origin).wait_recv()

            @pl.when(z > 0)
            def _():
                down(origin).start()

            side(origin).start()
            transpose(origin, c)

    def weights_first(j):
        copies = []
        for o in range(1, nx):
            for w in (w_in, w_out):
                copies.append(push(w.at[j, y, x, 0], w.at[j, y, x, 0], on_x(o)))
        for o in range(1, ny):
            for w in (w_in, w_out):
                copies.append(push(w.at[j, y, x, 1], w.at[j, y, x, 1], on_y(o)))
        return copies

    def weights_second(j):
        copies = []
        for o in range(1, ny):
            for w in (w_in, w_out):
                copies.append(push(w.at[j, y, :, 0], w.at[j, y, :, 0], on_y(o)))
        for o in range(1, nx):
            for w in (w_in, w_out):
                copies.append(push(w.at[j, :, x, 1], w.at[j, :, x, 1], on_x(o)))
        return copies

    for copy in own:
        copy.wait()
    first0 = weights_first(0)

    @pl.when(z < nz - 1)
    def _():
        up(z).start()

    @pl.when(z > 0)
    def _():
        down(z).start()

    side(z).start()
    transpose(z, c)
    arrived(first0)
    second0 = weights_second(0)

    def forward(j, first, group):
        rows = group * 2 * tok
        glane = lax.broadcasted_iota(jnp.int32, (rows, LANES), 1)
        at = pl.ds(first, group)
        gates = blocks[at, :, :, 2 * width :].reshape(rows, LANES).astype(F32)
        mine = glane == EXP_DEV * me + j
        g = jnp.sum(jnp.where(mine, gates, 0.0), axis=1, keepdims=True)
        pre_act = dot(
            blocks[at, :, :, :width].reshape(rows, width), w_in[j].reshape(width, cols_in)
        )
        raw = dot_nt(
            blocks[at, :, :, width : 2 * width].reshape(rows, width),
            w_out[j].reshape(hidden, width),
        )
        gate_pre, up_pre = pre_act[:, :hidden], pre_act[:, hidden:]
        sig = jax.nn.sigmoid(gate_pre)
        silu = gate_pre * sig
        act = silu * up_pre
        act_grad = g * raw
        r = pl.ds(pl.multiple_of(first * (2 * tok), 2 * tok), rows)
        pre[j, r, :hidden] = (act_grad * up_pre * sig * (1.0 + gate_pre * (1.0 - sig))).astype(BF16)
        pre[j, r, hidden:] = (act_grad * silu).astype(BF16)
        act_t[:, r] = (g * act).astype(BF16).T
        sums = jnp.sum(act * raw, axis=1, keepdims=True)
        placed = jnp.where(mine, sums, 0.0)
        if j > 0:
            placed += dxp[at, :, :, width:].reshape(rows, LANES).astype(F32)
        dxp[at, :, :, width:] = placed.astype(BF16).reshape(group, 2, tok, LANES)

    near = jnp.minimum(z, nz - 1 - z)

    def by_distance(n):
        s = (n + 1) // 2
        close = jnp.where(n % 2 == 1, z - s, z + s)
        far = jnp.where(z == near, n, nz - 1 - n)
        return jnp.where(n <= 2 * near, close, far)

    def forward_arrived(n, carry):
        origin = by_distance(n)
        side(origin).wait_recv()
        transpose(origin, 1 - c)
        forward(0, origin, 1)
        return carry

    group = min(nz, max(1, 512 // (2 * tok)))
    rows = group * 2 * tok

    def forward_all(i, carry):
        forward(1, i * group, group)
        return carry

    def gradients_in(j):
        def step(yy, carry):
            r_in = nx * rows_in
            part = dot(x_t[pl.ds(pl.multiple_of(yy * r_in, r_in), r_in), :], pre[j])
            g_in[j, yy] = part.astype(BF16).reshape(nx, 2, half_in, cols_in)
            return carry

        lax.fori_loop(0, ny, step, 0)

    def gradients_out(j):
        def step(yy, carry):
            r_out = nx * rows_out
            part = dot(
                act_t[pl.ds(pl.multiple_of(yy * r_out, r_out), r_out), :],
                blocks[:, :, :, width : 2 * width].reshape(total, width),
            )
            g_out[j, yy] = part.astype(BF16).reshape(nx, 2, half_out, width)
            return carry

        lax.fori_loop(0, ny, step, 0)

    kinds = (
        (g_in, in_r1a, in_r1b, in_r2a, in_r2b, ggu_ref, half_in),
        (g_out, out_r1a, out_r1b, out_r2a, out_r2b, gd_ref, half_out),
    )

    def sums_first(j, kind):
        grad, r1a, r1b = kind[:3]
        along_y, along_x = [], []
        for o in range(1, ny):
            to = lax.rem(y + o, ny)
            along_y.append(push(grad.at[j, to, :, 0], r1a.at[j, o - 1], on_y(o)))
        for o in range(1, nx):
            to = lax.rem(x + o, nx)
            along_x.append(push(grad.at[j, :, to, 1], r1b.at[j, o - 1], on_x(o)))
        return along_y, along_x

    def sums_second(j, kind, firsts):
        grad, r1a, r1b, r2a, r2b, out, half = kind
        along_x, along_y = [], []
        arrived(firsts[0])
        for o in reversed(range(nx)):
            to = lax.rem(x + o, nx)
            value = grad[j, y, to, 0].astype(F32)
            for n in range(ny - 1):
                value += r1a[j, n, to].astype(F32)
            if o == 0:
                out[j, :half] = value
            else:
                grad[j, y, to, 0] = value.astype(BF16)
                along_x.append(push(grad.at[j, y, to, 0], r2a.at[j, o - 1], on_x(o)))
        arrived(firsts[1])
        for o in reversed(range(ny)):
            to = lax.rem(y + o, ny)
            value = grad[j, to, x, 1].astype(F32)
            for n in range(nx - 1):
                value += r1b[j, n, to].astype(F32)
            if o == 0:
                out[j, half:] = value
            else:
                grad[j, to, x, 1] = value.astype(BF16)
                along_y.append(push(grad.at[j, to, x, 1], r2b.at[j, o - 1], on_y(o)))
        return along_x, along_y

    def sums_last(j, kind, seconds):
        r2a, r2b, out, half = kind[3:]
        arrived(seconds[0])
        value = out[j, :half]
        for n in range(nx - 1):
            value += r2a[j, n].astype(F32)
        out[j, :half] = value
        arrived(seconds[1])
        value = out[j, half:]
        for n in range(ny - 1):
            value += r2b[j, n].astype(F32)
        out[j, half:] = value

    for s in range(1, nz - 1):
        chain_step(s)
    arrived(second0)
    first1 = weights_first(1)
    lax.fori_loop(0, nz - 1, forward_arrived, 0)
    arrived(first1)
    second1 = weights_second(1)
    chain_step(nz - 1)
    forward_arrived(nz - 1, 0)
    gradients_in(0)
    firsts0 = [sums_first(0, kinds[0])]
    gradients_out(0)
    firsts0.append(sums_first(0, kinds[1]))
    arrived(second1)
    lax.fori_loop(0, nz // group, forward_all, 0)
    gradients_in(1)
    firsts1 = [sums_first(1, kinds[0])]
    gradients_out(1)
    firsts1.append(sums_first(1, kinds[1]))

    def dx_pair(to):
        return pltpu.make_async_remote_copy(
            src_ref=dxp.at[to, 1 - c], dst_ref=dx_r1.at[to],
            send_sem=dxp_send.at[to], recv_sem=dxp_recv.at[to],
            device_id=partner, device_id_type=pl.DeviceIdType.MESH,
        )

    def dx_spread(to, slot):
        return pltpu.make_async_remote_copy(
            src_ref=dxp.at[to, c], dst_ref=dx_r2.at[slot],
            send_sem=dxs_send.at[to], recv_sem=dxs_recv.at[slot],
            device_id=on_z(to), device_id_type=pl.DeviceIdType.MESH,
        )

    def dx_step(i, carry):
        to = lax.rem(z + 1 + i, nz)
        r = pl.ds(pl.multiple_of(to * (2 * tok), 2 * tok), 2 * tok)
        value = dot_nt(pre[0, r, :], w_in[0].reshape(width, cols_in))
        value += dot_nt(pre[1, r, :], w_in[1].reshape(width, cols_in))
        dxp[to, :, :, :width] = value.astype(BF16).reshape(2, tok, width)
        dx_pair(to).start()

        @pl.when(i > 0)
        def _():
            last = lax.rem(z + i, nz)
            dx_pair(last).wait_recv()
            dxp[last, c] = (dxp[last, c].astype(F32) + dx_r1[last].astype(F32)).astype(BF16)
            dx_spread(last, z).start()

        return carry

    lax.fori_loop(0, nz, dx_step, 0)
    seconds0 = [sums_second(0, kind, first) for kind, first in zip(kinds, firsts0)]
    seconds1 = [sums_second(1, kind, first) for kind, first in zip(kinds, firsts1)]
    for kind, second in zip(kinds, seconds0):
        sums_last(0, kind, second)

    dx_pair(z).wait_recv()
    value = dxp[z, c].astype(F32) + dx_r1[z].astype(F32)
    for o in range(1, nz):
        source = lax.rem(z + o, nz)
        dx_spread(source, source).wait_recv()
        value += dx_r2[source].astype(F32)
    gtok_ref[...] = value[:, :width].astype(BF16)
    back = value[:, width:].T
    for k in range(top):
        ggate_ref[k : k + 1, :] = jnp.sum(
            jnp.where(ids[k : k + 1] == expert, back, 0.0), axis=0, keepdims=True
        )

    for kind, second in zip(kinds, seconds1):
        sums_last(1, kind, second)

    for copy in started:
        copy.wait_send()

    def drain(origin):
        side(origin).wait_send()
        dx_pair(origin).wait_send()

        @pl.when(origin != z)
        def _():
            dx_spread(origin, z).wait_send()

        @pl.when((origin <= z) & (z < nz - 1))
        def _():
            up(origin).wait_send()

        @pl.when((origin >= z) & (z > 0))
        def _():
            down(origin).wait_send()

    for zz in range(nz):
        drain(zz)


def emit(gtok, ggu, gd, gtok_out, ggu_out, gd_out, gtok_v, ggu_v, gd_v, sems_in, sems_out):
    parts = [(gtok, gtok_v, gtok_out)]
    for j in range(EXP_DEV):
        for src, mid, dst in ((ggu, ggu_v, ggu_out), (gd, gd_v, gd_out)):
            half = src.shape[1] // 2
            for h in range(2):
                at = pl.ds(h * half, half)
                parts.append((src.at[j, at], mid.at[j, at], dst.at[j, at]))
    ins = [pltpu.make_async_copy(s, m, sems_in.at[i]) for i, (s, m, _) in enumerate(parts)]
    outs = [pltpu.make_async_copy(m, d, sems_out.at[i]) for i, (_, m, d) in enumerate(parts)]
    for copy in ins:
        copy.start()
    for first, second in zip(ins, outs):
        first.wait()
        second.start()
    for copy in outs:
        copy.wait()


def body(ny, nx, nz, tokens, cotangent, expert_ids, gate_probs, gate_up, down_proj):
    tok, width = tokens.shape
    rows_in, cols_in = gate_up.shape[1:]
    rows_out = down_proj.shape[1]
    hi, ho = rows_in // 2, rows_out // 2
    total = nz * 2 * tok
    copies = 16 * (nx + ny - 2)
    V = pltpu.VMEM
    dma = pltpu.SemaphoreType.DMA
    e = EXP_DEV
    flops = 2 * e * total * width * cols_in * 4
    gtok, ggate, ggu, gd = pl.pallas_call(
        functools.partial(kernel, ny, nx, nz),
        out_shape=(
            jax.ShapeDtypeStruct(tokens.shape, BF16),
            jax.ShapeDtypeStruct(gate_probs.shape[::-1], F32),
            jax.ShapeDtypeStruct(gate_up.shape, F32),
            jax.ShapeDtypeStruct(down_proj.shape, F32),
        ),
        in_specs=[pl.BlockSpec(memory_space=V)] * 4 + [pl.BlockSpec(memory_space=pl.ANY)] * 2,
        out_specs=[pl.BlockSpec(memory_space=V)] * 4,
        scratch_shapes=[
            V((nz, 2, tok, 2 * width + LANES), BF16),
            V((width, total), BF16),
            V((e, ny, nx, 2, hi, cols_in), BF16),
            V((e, ny, nx, 2, ho, width), BF16),
            V((e, total, cols_in), BF16),
            V((cols_in // 2, total), BF16),
            V((e, ny, nx, 2, hi, cols_in), BF16),
            V((e, ny, nx, 2, ho, width), BF16),
            V((e, ny - 1, nx, hi, cols_in), BF16),
            V((e, nx - 1, ny, hi, cols_in), BF16),
            V((e, nx - 1, hi, cols_in), BF16),
            V((e, ny - 1, hi, cols_in), BF16),
            V((e, ny - 1, nx, ho, width), BF16),
            V((e, nx - 1, ny, ho, width), BF16),
            V((e, nx - 1, ho, width), BF16),
            V((e, ny - 1, ho, width), BF16),
            V((nz, 2, tok, width + LANES), BF16),
            V((nz, tok, width + LANES), BF16),
            V((nz, tok, width + LANES), BF16),
            dma((copies,)),
            dma((copies,)),
            dma((nz,)),
            dma((nz,)),
            dma((nz,)),
            dma((nz,)),
            dma((nz,)),
            dma((4,)),
            dma((nz,)),
            dma((nz,)),
            dma((nz,)),
            dma((nz,)),
        ],
        compiler_params=pltpu.CompilerParams(
            collective_id=0, has_side_effects=True, vmem_limit_bytes=60 * 2**20
        ),
        cost_estimate=pl.CostEstimate(flops=flops, bytes_accessed=8 * 2**20, transcendentals=0),
    )(
        tokens, cotangent, expert_ids.T, gate_probs.T,
        gate_up.reshape(e, 2, hi, cols_in), down_proj.reshape(e, 2, ho, width),
    )
    gtok, ggu, gd = pl.pallas_call(
        emit,
        out_shape=tuple(jax.ShapeDtypeStruct(a.shape, a.dtype) for a in (gtok, ggu, gd)),
        in_specs=[pl.BlockSpec(memory_space=pl.ANY)] * 3,
        out_specs=[pl.BlockSpec(memory_space=pl.ANY)] * 3,
        scratch_shapes=[V(a.shape, a.dtype) for a in (gtok, ggu, gd)] + [dma((4 * e + 1,))] * 2,
        compiler_params=pltpu.CompilerParams(vmem_limit_bytes=60 * 2**20),
    )(gtok, ggu, gd)
    return gtok, ggate.astype(BF16).T, ggu, gd


def solution(mesh):
    dp = mesh.shape["dp"]
    nx = next(n for n in range(math.isqrt(dp), 0, -1) if dp % n == 0)
    tok = P(("dp", "expert"), None)
    wgt = P("expert", "dp", None)
    return jax.shard_map(
        functools.partial(body, dp // nx, nx, mesh.shape["expert"] // 2),
        mesh=mesh,
        in_specs=(tok, tok, tok, tok, wgt, wgt),
        out_specs=(tok, tok, wgt, wgt),
        check_vma=False,
    )
```

```python
import functools
import math

import jax
import jax.numpy as jnp
from jax import lax
from jax.experimental import pallas as pl
from jax.experimental.pallas import tpu as pltpu
from jax.sharding import PartitionSpec as P

EXP_DEV = 2
LANES = 128
BF16 = jnp.bfloat16
F32 = jnp.float32


def dot(a, b):
    return jnp.dot(a, b, preferred_element_type=F32)


def dot_nt(a, b):
    return lax.dot_general(a, b, (((1,), (1,)), ((), ())), preferred_element_type=F32)


def kernel(
    ny, nx, nz,
    x_ref, dy_ref, ids_ref, gates_ref, wgu_ref, wd_ref,
    gtok_ref, ggate_ref, ggu_ref, gd_ref,
    blocks, x_t, w_in, w_out, pre, act_t, g_in, g_out,
    in_r1a, in_r1b, in_r2a, in_r2b, out_r1a, out_r1b, out_r2a, out_r2b,
    dxp, dx_r1, dx_r2,
    send_sems, recv_sems, up_sems, down_sems, side_sems, chain_sems, pair_sems, own_sems,
    dxp_send, dxp_recv, dxs_send, dxs_recv,
):
    dp, me = lax.axis_index("dp"), lax.axis_index("expert")
    y, x = dp // nx, dp % nx
    z, c = me // 2, me % 2
    tok, width = x_ref.shape
    half_in, cols_in = wgu_ref.shape[2:]
    half_out = wd_ref.shape[2]
    rows_in, rows_out = 2 * half_in, 2 * half_out
    hidden = cols_in // 2
    total = nz * 2 * tok
    top = ids_ref.shape[0]

    def on_y(o):
        return (lax.rem(y + o, ny) * nx + x, me)

    def on_x(o):
        return (y * nx + lax.rem(x + o, nx), me)

    def on_z(zz):
        return (dp, zz * 2 + c)

    partner = (dp, z * 2 + 1 - c)
    peers = [on_y(o) for o in range(1, ny)] + [on_x(o) for o in range(1, nx)]
    peers += [on_z(lax.rem(z + o, nz)) for o in range(1, nz)] + [partner]

    barrier = pltpu.get_barrier_semaphore()
    for peer in peers:
        pl.semaphore_signal(barrier, inc=1, device_id=peer, device_id_type=pl.DeviceIdType.MESH)

    own = []
    for j in range(EXP_DEV):
        own.append(pltpu.make_async_copy(wgu_ref.at[j], w_in.at[j, y, x], own_sems.at[2 * j]))
        own.append(pltpu.make_async_copy(wd_ref.at[j], w_out.at[j, y, x], own_sems.at[2 * j + 1]))
    for copy in own:
        copy.start()

    expert = lax.broadcasted_iota(jnp.int32, (LANES, tok), 0)
    ids = ids_ref[...]
    gate_rows = gates_ref[...].astype(F32)
    dense = jnp.zeros((LANES, tok), F32)
    for k in range(top):
        dense += jnp.where(ids[k : k + 1] == expert, gate_rows[k : k + 1], 0.0)
    blocks[z, c, :, :width] = x_ref[...]
    blocks[z, c, :, width : 2 * width] = dy_ref[...]
    blocks[z, c, :, 2 * width :] = dense.T.astype(BF16)

    pl.semaphore_wait(barrier, len(peers))

    started = []

    def push(src, dst, peer):
        i = len(started)
        copy = pltpu.make_async_remote_copy(
            src_ref=src, dst_ref=dst, send_sem=send_sems.at[i], recv_sem=recv_sems.at[i],
            device_id=peer, device_id_type=pl.DeviceIdType.MESH,
        )
        copy.start()
        started.append(copy)
        return copy

    def arrived(copies):
        for copy in copies:
            copy.wait_recv()

    def block_copy(origin, send_sem, recv_sem, peer):
        ref = blocks.at[origin, c]
        return pltpu.make_async_remote_copy(
            src_ref=ref, dst_ref=ref, send_sem=send_sem, recv_sem=recv_sem,
            device_id=peer, device_id_type=pl.DeviceIdType.MESH,
        )

    def up(origin):
        peer = on_z(jnp.minimum(z + 1, nz - 1))
        return block_copy(origin, up_sems.at[origin], chain_sems.at[origin], peer)

    def down(origin):
        peer = on_z(jnp.maximum(z - 1, 0))
        return block_copy(origin, down_sems.at[origin], chain_sems.at[origin], peer)

    def side(origin):
        return block_copy(origin, side_sems.at[origin], pair_sems.at[origin], partner)

    def transpose(zz, cc):
        at = pl.multiple_of((zz * 2 + cc) * tok, tok)
        x_t[:, pl.ds(at, tok)] = blocks[zz, cc, :, :width].T

    def chain_step(s):
        @pl.when(z - s >= 0)
        def _():
            origin = z - s
            up(origin).wait_recv()

            @pl.when(z < nz - 1)
            def _():
                up(origin).start()

            side(origin).start()
            transpose(origin, c)

        @pl.when(z + s < nz)
        def _():
            origin = z + s
            down(origin).wait_recv()

            @pl.when(z > 0)
            def _():
                down(origin).start()

            side(origin).start()
            transpose(origin, c)

    def weights_first(j):
        copies = []
        for o in range(1, nx):
            for w in (w_in, w_out):
                copies.append(push(w.at[j, y, x, 0], w.at[j, y, x, 0], on_x(o)))
        for o in range(1, ny):
            for w in (w_in, w_out):
                copies.append(push(w.at[j, y, x, 1], w.at[j, y, x, 1], on_y(o)))
        return copies

    def weights_second(j):
        copies = []
        for o in range(1, ny):
            for w in (w_in, w_out):
                copies.append(push(w.at[j, y, :, 0], w.at[j, y, :, 0], on_y(o)))
        for o in range(1, nx):
            for w in (w_in, w_out):
                copies.append(push(w.at[j, :, x, 1], w.at[j, :, x, 1], on_x(o)))
        return copies

    for copy in own:
        copy.wait()
    first0 = weights_first(0)

    @pl.when(z < nz - 1)
    def _():
        up(z).start()

    @pl.when(z > 0)
    def _():
        down(z).start()

    side(z).start()
    transpose(z, c)
    arrived(first0)
    second0 = weights_second(0)

    def forward(j, first, group):
        rows = group * 2 * tok
        glane = lax.broadcasted_iota(jnp.int32, (rows, LANES), 1)
        at = pl.ds(first, group)
        gates = blocks[at, :, :, 2 * width :].reshape(rows, LANES).astype(F32)
        mine = glane == EXP_DEV * me + j
        g = jnp.sum(jnp.where(mine, gates, 0.0), axis=1, keepdims=True)
        pre_act = dot(
            blocks[at, :, :, :width].reshape(rows, width), w_in[j].reshape(width, cols_in)
        )
        raw = dot_nt(
            blocks[at, :, :, width : 2 * width].reshape(rows, width),
            w_out[j].reshape(hidden, width),
        )
        gate_pre, up_pre = pre_act[:, :hidden], pre_act[:, hidden:]
        sig = jax.nn.sigmoid(gate_pre)
        silu = gate_pre * sig
        act = silu * up_pre
        act_grad = g * raw
        r = pl.ds(pl.multiple_of(first * (2 * tok), 2 * tok), rows)
        pre[j, r, :hidden] = (act_grad * up_pre * sig * (1.0 + gate_pre * (1.0 - sig))).astype(BF16)
        pre[j, r, hidden:] = (act_grad * silu).astype(BF16)
        act_t[:, r] = (g * act).astype(BF16).T
        sums = jnp.sum(act * raw, axis=1, keepdims=True)
        placed = jnp.where(mine, sums, 0.0)
        if j > 0:
            placed += dxp[at, :, :, width:].reshape(rows, LANES).astype(F32)
        dxp[at, :, :, width:] = placed.astype(BF16).reshape(group, 2, tok, LANES)

    near = jnp.minimum(z, nz - 1 - z)

    def by_distance(n):
        s = (n + 1) // 2
        close = jnp.where(n % 2 == 1, z - s, z + s)
        far = jnp.where(z == near, n, nz - 1 - n)
        return jnp.where(n <= 2 * near, close, far)

    def forward_arrived(n, carry):
        origin = by_distance(n)
        side(origin).wait_recv()
        transpose(origin, 1 - c)
        forward(0, origin, 1)
        return carry

    group = min(nz, max(1, 512 // (2 * tok)))
    rows = group * 2 * tok

    def forward_all(i, carry):
        forward(1, i * group, group)
        return carry

    def gradients_in(j):
        def step(yy, carry):
            r_in = nx * rows_in
            part = dot(x_t[pl.ds(pl.multiple_of(yy * r_in, r_in), r_in), :], pre[j])
            g_in[j, yy] = part.astype(BF16).reshape(nx, 2, half_in, cols_in)
            return carry

        lax.fori_loop(0, ny, step, 0)

    def gradients_out(j):
        def step(yy, carry):
            r_out = nx * rows_out
            part = dot(
                act_t[pl.ds(pl.multiple_of(yy * r_out, r_out), r_out), :],
                blocks[:, :, :, width : 2 * width].reshape(total, width),
            )
            g_out[j, yy] = part.astype(BF16).reshape(nx, 2, half_out, width)
            return carry

        lax.fori_loop(0, ny, step, 0)

    kinds = (
        (g_in, in_r1a, in_r1b, in_r2a, in_r2b, ggu_ref, half_in),
        (g_out, out_r1a, out_r1b, out_r2a, out_r2b, gd_ref, half_out),
    )

    def sums_first(j, kind):
        grad, r1a, r1b = kind[:3]
        along_y, along_x = [], []
        for o in range(1, ny):
            to = lax.rem(y + o, ny)
            along_y.append(push(grad.at[j, to, :, 0], r1a.at[j, o - 1], on_y(o)))
        for o in range(1, nx):
            to = lax.rem(x + o, nx)
            along_x.append(push(grad.at[j, :, to, 1], r1b.at[j, o - 1], on_x(o)))
        return along_y, along_x

    def sums_second(j, kind, firsts):
        grad, r1a, r1b, r2a, r2b, out, half = kind
        along_x, along_y = [], []
        arrived(firsts[0])
        for o in reversed(range(nx)):
            to = lax.rem(x + o, nx)
            value = grad[j, y, to, 0].astype(F32)
            for n in range(ny - 1):
                value += r1a[j, n, to].astype(F32)
            if o == 0:
                out[j, :half] = value
            else:
                grad[j, y, to, 0] = value.astype(BF16)
                along_x.append(push(grad.at[j, y, to, 0], r2a.at[j, o - 1], on_x(o)))
        arrived(firsts[1])
        for o in reversed(range(ny)):
            to = lax.rem(y + o, ny)
            value = grad[j, to, x, 1].astype(F32)
            for n in range(nx - 1):
                value += r1b[j, n, to].astype(F32)
            if o == 0:
                out[j, half:] = value
            else:
                grad[j, to, x, 1] = value.astype(BF16)
                along_y.append(push(grad.at[j, to, x, 1], r2b.at[j, o - 1], on_y(o)))
        return along_x, along_y

    def sums_last(j, kind, seconds):
        r2a, r2b, out, half = kind[3:]
        arrived(seconds[0])
        value = out[j, :half]
        for n in range(nx - 1):
            value += r2a[j, n].astype(F32)
        out[j, :half] = value
        arrived(seconds[1])
        value = out[j, half:]
        for n in range(ny - 1):
            value += r2b[j, n].astype(F32)
        out[j, half:] = value

    for s in range(1, nz - 1):
        chain_step(s)
    arrived(second0)
    first1 = weights_first(1)
    lax.fori_loop(0, nz - 2, forward_arrived, 0)
    arrived(first1)
    second1 = weights_second(1)
    forward_arrived(nz - 2, 0)
    chain_step(nz - 1)
    forward_arrived(nz - 1, 0)
    gradients_in(0)
    firsts0 = [sums_first(0, kinds[0])]
    gradients_out(0)
    firsts0.append(sums_first(0, kinds[1]))
    arrived(second1)
    lax.fori_loop(0, nz // group, forward_all, 0)
    gradients_in(1)
    firsts1 = [sums_first(1, kinds[0])]
    def dx_pair(to):
        return pltpu.make_async_remote_copy(
            src_ref=dxp.at[to, 1 - c], dst_ref=dx_r1.at[to],
            send_sem=dxp_send.at[to], recv_sem=dxp_recv.at[to],
            device_id=partner, device_id_type=pl.DeviceIdType.MESH,
        )

    def dx_spread(to, slot):
        return pltpu.make_async_remote_copy(
            src_ref=dxp.at[to, c], dst_ref=dx_r2.at[slot],
            send_sem=dxs_send.at[to], recv_sem=dxs_recv.at[slot],
            device_id=on_z(to), device_id_type=pl.DeviceIdType.MESH,
        )

    def dx_step(i, carry):
        to = lax.rem(z + 1 + i, nz)
        r = pl.ds(pl.multiple_of(to * (2 * tok), 2 * tok), 2 * tok)
        value = dot_nt(pre[0, r, :], w_in[0].reshape(width, cols_in))
        value += dot_nt(pre[1, r, :], w_in[1].reshape(width, cols_in))
        dxp[to, :, :, :width] = value.astype(BF16).reshape(2, tok, width)
        dx_pair(to).start()

        @pl.when(i > 0)
        def _():
            last = lax.rem(z + i, nz)
            dx_pair(last).wait_recv()
            dxp[last, c] = (dxp[last, c].astype(F32) + dx_r1[last].astype(F32)).astype(BF16)
            dx_spread(last, z).start()

        return carry

    lax.fori_loop(0, nz, dx_step, 0)
    seconds0 = [sums_second(0, kinds[0], firsts0[0])]
    gradients_out(1)
    firsts1.append(sums_first(1, kinds[1]))
    seconds0.append(sums_second(0, kinds[1], firsts0[1]))
    seconds1 = [sums_second(1, kind, first) for kind, first in zip(kinds, firsts1)]
    for kind, second in zip(kinds, seconds0):
        sums_last(0, kind, second)

    dx_pair(z).wait_recv()
    value = dxp[z, c].astype(F32) + dx_r1[z].astype(F32)
    for o in range(1, nz):
        source = lax.rem(z + o, nz)
        dx_spread(source, source).wait_recv()
        value += dx_r2[source].astype(F32)
    gtok_ref[...] = value[:, :width].astype(BF16)
    back = value[:, width:].T
    for k in range(top):
        ggate_ref[k : k + 1, :] = jnp.sum(
            jnp.where(ids[k : k + 1] == expert, back, 0.0), axis=0, keepdims=True
        )

    for kind, second in zip(kinds, seconds1):
        sums_last(1, kind, second)

    for copy in started:
        copy.wait_send()

    def drain(origin):
        side(origin).wait_send()
        dx_pair(origin).wait_send()

        @pl.when(origin != z)
        def _():
            dx_spread(origin, z).wait_send()

        @pl.when((origin <= z) & (z < nz - 1))
        def _():
            up(origin).wait_send()

        @pl.when((origin >= z) & (z > 0))
        def _():
            down(origin).wait_send()

    for zz in range(nz):
        drain(zz)


def emit(gtok, ggu, gd, gtok_out, ggu_out, gd_out, gtok_v, ggu_v, gd_v, sems_in, sems_out):
    parts = [(gtok, gtok_v, gtok_out)]
    for j in range(EXP_DEV):
        for src, mid, dst in ((ggu, ggu_v, ggu_out), (gd, gd_v, gd_out)):
            half = src.shape[1] // 2
            for h in range(2):
                at = pl.ds(h * half, half)
                parts.append((src.at[j, at], mid.at[j, at], dst.at[j, at]))
    ins = [pltpu.make_async_copy(s, m, sems_in.at[i]) for i, (s, m, _) in enumerate(parts)]
    outs = [pltpu.make_async_copy(m, d, sems_out.at[i]) for i, (_, m, d) in enumerate(parts)]
    for copy in ins:
        copy.start()
    for first, second in zip(ins, outs):
        first.wait()
        second.start()
    for copy in outs:
        copy.wait()


def body(ny, nx, nz, tokens, cotangent, expert_ids, gate_probs, gate_up, down_proj):
    tok, width = tokens.shape
    rows_in, cols_in = gate_up.shape[1:]
    rows_out = down_proj.shape[1]
    hi, ho = rows_in // 2, rows_out // 2
    total = nz * 2 * tok
    copies = 16 * (nx + ny - 2)
    V = pltpu.VMEM
    dma = pltpu.SemaphoreType.DMA
    e = EXP_DEV
    flops = 2 * e * total * width * cols_in * 4
    gtok, ggate, ggu, gd = pl.pallas_call(
        functools.partial(kernel, ny, nx, nz),
        out_shape=(
            jax.ShapeDtypeStruct(tokens.shape, BF16),
            jax.ShapeDtypeStruct(gate_probs.shape[::-1], F32),
            jax.ShapeDtypeStruct(gate_up.shape, F32),
            jax.ShapeDtypeStruct(down_proj.shape, F32),
        ),
        in_specs=[pl.BlockSpec(memory_space=V)] * 4 + [pl.BlockSpec(memory_space=pl.ANY)] * 2,
        out_specs=[pl.BlockSpec(memory_space=V)] * 4,
        scratch_shapes=[
            V((nz, 2, tok, 2 * width + LANES), BF16),
            V((width, total), BF16),
            V((e, ny, nx, 2, hi, cols_in), BF16),
            V((e, ny, nx, 2, ho, width), BF16),
            V((e, total, cols_in), BF16),
            V((cols_in // 2, total), BF16),
            V((e, ny, nx, 2, hi, cols_in), BF16),
            V((e, ny, nx, 2, ho, width), BF16),
            V((e, ny - 1, nx, hi, cols_in), BF16),
            V((e, nx - 1, ny, hi, cols_in), BF16),
            V((e, nx - 1, hi, cols_in), BF16),
            V((e, ny - 1, hi, cols_in), BF16),
            V((e, ny - 1, nx, ho, width), BF16),
            V((e, nx - 1, ny, ho, width), BF16),
            V((e, nx - 1, ho, width), BF16),
            V((e, ny - 1, ho, width), BF16),
            V((nz, 2, tok, width + LANES), BF16),
            V((nz, tok, width + LANES), BF16),
            V((nz, tok, width + LANES), BF16),
            dma((copies,)),
            dma((copies,)),
            dma((nz,)),
            dma((nz,)),
            dma((nz,)),
            dma((nz,)),
            dma((nz,)),
            dma((4,)),
            dma((nz,)),
            dma((nz,)),
            dma((nz,)),
            dma((nz,)),
        ],
        compiler_params=pltpu.CompilerParams(
            collective_id=0, has_side_effects=True, vmem_limit_bytes=60 * 2**20
        ),
        cost_estimate=pl.CostEstimate(flops=flops, bytes_accessed=8 * 2**20, transcendentals=0),
    )(
        tokens, cotangent, expert_ids.T, gate_probs.T,
        gate_up.reshape(e, 2, hi, cols_in), down_proj.reshape(e, 2, ho, width),
    )
    gtok, ggu, gd = pl.pallas_call(
        emit,
        out_shape=tuple(jax.ShapeDtypeStruct(a.shape, a.dtype) for a in (gtok, ggu, gd)),
        in_specs=[pl.BlockSpec(memory_space=pl.ANY)] * 3,
        out_specs=[pl.BlockSpec(memory_space=pl.ANY)] * 3,
        scratch_shapes=[V(a.shape, a.dtype) for a in (gtok, ggu, gd)] + [dma((4 * e + 1,))] * 2,
        compiler_params=pltpu.CompilerParams(vmem_limit_bytes=60 * 2**20),
    )(gtok, ggu, gd)
    return gtok, ggate.astype(BF16).T, ggu, gd


def solution(mesh):
    dp = mesh.shape["dp"]
    nx = next(n for n in range(math.isqrt(dp), 0, -1) if dp % n == 0)
    tok = P(("dp", "expert"), None)
    wgt = P("expert", "dp", None)
    return jax.shard_map(
        functools.partial(body, dp // nx, nx, mesh.shape["expert"] // 2),
        mesh=mesh,
        in_specs=(tok, tok, tok, tok, wgt, wgt),
        out_specs=(tok, tok, wgt, wgt),
        check_vma=False,
    )
```

```python
import functools
import math

import jax
import jax.numpy as jnp
from jax import lax
from jax.experimental import pallas as pl
from jax.experimental.pallas import tpu as pltpu
from jax.sharding import PartitionSpec as P

EXP_DEV = 2
LANES = 128
BF16 = jnp.bfloat16
F32 = jnp.float32


def dot(a, b):
    return jnp.dot(a, b, preferred_element_type=F32)


def dot_nt(a, b):
    return lax.dot_general(a, b, (((1,), (1,)), ((), ())), preferred_element_type=F32)


def kernel(
    ny, nx, nz,
    x_ref, dy_ref, ids_ref, gates_ref, wgu_ref, wd_ref,
    gtok_ref, ggate_ref, ggu_ref, gd_ref,
    blocks, x_t, w_in, w_out, pre, act_t, g_in, g_out,
    in_r1a, in_r1b, in_r2a, in_r2b, out_r1a, out_r1b, out_r2a, out_r2b,
    dxp, dx_r1, dx_r2,
    send_sems, recv_sems, up_sems, down_sems, side_sems, chain_sems, pair_sems, own_sems,
    dxp_send, dxp_recv, dxs_send, dxs_recv,
):
    dp, me = lax.axis_index("dp"), lax.axis_index("expert")
    y, x = dp // nx, dp % nx
    z, c = me // 2, me % 2
    tok, width = x_ref.shape
    half_in, cols_in = wgu_ref.shape[2:]
    half_out = wd_ref.shape[2]
    rows_in, rows_out = 2 * half_in, 2 * half_out
    hidden = cols_in // 2
    total = nz * 2 * tok
    top = ids_ref.shape[0]

    def on_y(o):
        return (lax.rem(y + o, ny) * nx + x, me)

    def on_x(o):
        return (y * nx + lax.rem(x + o, nx), me)

    def on_z(zz):
        return (dp, zz * 2 + c)

    partner = (dp, z * 2 + 1 - c)
    peers = [on_y(o) for o in range(1, ny)] + [on_x(o) for o in range(1, nx)]
    peers += [on_z(lax.rem(z + o, nz)) for o in range(1, nz)] + [partner]

    barrier = pltpu.get_barrier_semaphore()
    for peer in peers:
        pl.semaphore_signal(barrier, inc=1, device_id=peer, device_id_type=pl.DeviceIdType.MESH)

    own = []
    for j in range(EXP_DEV):
        own.append(pltpu.make_async_copy(wgu_ref.at[j], w_in.at[j, y, x], own_sems.at[2 * j]))
        own.append(pltpu.make_async_copy(wd_ref.at[j], w_out.at[j, y, x], own_sems.at[2 * j + 1]))
    for copy in own:
        copy.start()

    expert = lax.broadcasted_iota(jnp.int32, (LANES, tok), 0)
    ids = ids_ref[...]
    gate_rows = gates_ref[...].astype(F32)
    dense = jnp.zeros((LANES, tok), F32)
    for k in range(top):
        dense += jnp.where(ids[k : k + 1] == expert, gate_rows[k : k + 1], 0.0)
    blocks[z, c, :, :width] = x_ref[...]
    blocks[z, c, :, width : 2 * width] = dy_ref[...]
    blocks[z, c, :, 2 * width :] = dense.T.astype(BF16)

    pl.semaphore_wait(barrier, len(peers))

    started = []

    def push(src, dst, peer):
        i = len(started)
        copy = pltpu.make_async_remote_copy(
            src_ref=src, dst_ref=dst, send_sem=send_sems.at[i], recv_sem=recv_sems.at[i],
            device_id=peer, device_id_type=pl.DeviceIdType.MESH,
        )
        copy.start()
        started.append(copy)
        return copy

    def arrived(copies):
        for copy in copies:
            copy.wait_recv()

    def block_copy(origin, send_sem, recv_sem, peer):
        ref = blocks.at[origin, c]
        return pltpu.make_async_remote_copy(
            src_ref=ref, dst_ref=ref, send_sem=send_sem, recv_sem=recv_sem,
            device_id=peer, device_id_type=pl.DeviceIdType.MESH,
        )

    def up(origin):
        peer = on_z(jnp.minimum(z + 1, nz - 1))
        return block_copy(origin, up_sems.at[origin], chain_sems.at[origin], peer)

    def down(origin):
        peer = on_z(jnp.maximum(z - 1, 0))
        return block_copy(origin, down_sems.at[origin], chain_sems.at[origin], peer)

    def side(origin):
        return block_copy(origin, side_sems.at[origin], pair_sems.at[origin], partner)

    def transpose(zz, cc):
        at = pl.multiple_of((zz * 2 + cc) * tok, tok)
        x_t[:, pl.ds(at, tok)] = blocks[zz, cc, :, :width].T

    def chain_step(s):
        @pl.when(z - s >= 0)
        def _():
            origin = z - s
            up(origin).wait_recv()

            @pl.when(z < nz - 1)
            def _():
                up(origin).start()

            side(origin).start()
            transpose(origin, c)

        @pl.when(z + s < nz)
        def _():
            origin = z + s
            down(origin).wait_recv()

            @pl.when(z > 0)
            def _():
                down(origin).start()

            side(origin).start()
            transpose(origin, c)

    def weights_first(j):
        copies = []
        for o in range(1, nx):
            for w in (w_in, w_out):
                copies.append(push(w.at[j, y, x, 0], w.at[j, y, x, 0], on_x(o)))
        for o in range(1, ny):
            for w in (w_in, w_out):
                copies.append(push(w.at[j, y, x, 1], w.at[j, y, x, 1], on_y(o)))
        return copies

    def weights_second(j):
        copies = []
        for o in range(1, ny):
            for w in (w_in, w_out):
                copies.append(push(w.at[j, y, :, 0], w.at[j, y, :, 0], on_y(o)))
        for o in range(1, nx):
            for w in (w_in, w_out):
                copies.append(push(w.at[j, :, x, 1], w.at[j, :, x, 1], on_x(o)))
        return copies

    for copy in own:
        copy.wait()
    first0 = weights_first(0)

    @pl.when(z < nz - 1)
    def _():
        up(z).start()

    @pl.when(z > 0)
    def _():
        down(z).start()

    side(z).start()
    transpose(z, c)
    arrived(first0)
    second0 = weights_second(0)
    first1 = weights_first(1)

    def forward(j, first, group):
        rows = group * 2 * tok
        glane = lax.broadcasted_iota(jnp.int32, (rows, LANES), 1)
        at = pl.ds(first, group)
        gates = blocks[at, :, :, 2 * width :].reshape(rows, LANES).astype(F32)
        mine = glane == EXP_DEV * me + j
        g = jnp.sum(jnp.where(mine, gates, 0.0), axis=1, keepdims=True)
        pre_act = dot(
            blocks[at, :, :, :width].reshape(rows, width), w_in[j].reshape(width, cols_in)
        )
        raw = dot_nt(
            blocks[at, :, :, width : 2 * width].reshape(rows, width),
            w_out[j].reshape(hidden, width),
        )
        gate_pre, up_pre = pre_act[:, :hidden], pre_act[:, hidden:]
        sig = jax.nn.sigmoid(gate_pre)
        silu = gate_pre * sig
        act = silu * up_pre
        act_grad = g * raw
        r = pl.ds(pl.multiple_of(first * (2 * tok), 2 * tok), rows)
        pre[j, r, :hidden] = (act_grad * up_pre * sig * (1.0 + gate_pre * (1.0 - sig))).astype(BF16)
        pre[j, r, hidden:] = (act_grad * silu).astype(BF16)
        act_t[:, r] = (g * act).astype(BF16).T
        sums = jnp.sum(act * raw, axis=1, keepdims=True)
        placed = jnp.where(mine, sums, 0.0)
        if j > 0:
            placed += dxp[at, :, :, width:].reshape(rows, LANES).astype(F32)
        dxp[at, :, :, width:] = placed.astype(BF16).reshape(group, 2, tok, LANES)

    near = jnp.minimum(z, nz - 1 - z)

    def by_distance(n):
        s = (n + 1) // 2
        close = jnp.where(n % 2 == 1, z - s, z + s)
        far = jnp.where(z == near, n, nz - 1 - n)
        return jnp.where(n <= 2 * near, close, far)

    def forward_arrived(n, carry):
        origin = by_distance(n)
        side(origin).wait_recv()
        transpose(origin, 1 - c)
        forward(0, origin, 1)
        return carry

    group = min(nz, max(1, 512 // (2 * tok)))
    rows = group * 2 * tok

    def forward_all(i, carry):
        forward(1, i * group, group)
        return carry

    def gradients_in(j):
        def step(yy, carry):
            r_in = nx * rows_in
            part = dot(x_t[pl.ds(pl.multiple_of(yy * r_in, r_in), r_in), :], pre[j])
            g_in[j, yy] = part.astype(BF16).reshape(nx, 2, half_in, cols_in)
            return carry

        lax.fori_loop(0, ny, step, 0)

    def gradients_out(j):
        def step(yy, carry):
            r_out = nx * rows_out
            part = dot(
                act_t[pl.ds(pl.multiple_of(yy * r_out, r_out), r_out), :],
                blocks[:, :, :, width : 2 * width].reshape(total, width),
            )
            g_out[j, yy] = part.astype(BF16).reshape(nx, 2, half_out, width)
            return carry

        lax.fori_loop(0, ny, step, 0)

    kinds = (
        (g_in, in_r1a, in_r1b, in_r2a, in_r2b, ggu_ref, half_in),
        (g_out, out_r1a, out_r1b, out_r2a, out_r2b, gd_ref, half_out),
    )

    def sums_first(j, kind):
        grad, r1a, r1b = kind[:3]
        along_y, along_x = [], []
        for o in range(1, ny):
            to = lax.rem(y + o, ny)
            along_y.append(push(grad.at[j, to, :, 0], r1a.at[j, o - 1], on_y(o)))
        for o in range(1, nx):
            to = lax.rem(x + o, nx)
            along_x.append(push(grad.at[j, :, to, 1], r1b.at[j, o - 1], on_x(o)))
        return along_y, along_x

    def sums_second(j, kind, firsts):
        grad, r1a, r1b, r2a, r2b, out, half = kind
        along_x, along_y = [], []
        arrived(firsts[0])
        for o in reversed(range(nx)):
            to = lax.rem(x + o, nx)
            value = grad[j, y, to, 0].astype(F32)
            for n in range(ny - 1):
                value += r1a[j, n, to].astype(F32)
            if o == 0:
                out[j, :half] = value
            else:
                grad[j, y, to, 0] = value.astype(BF16)
                along_x.append(push(grad.at[j, y, to, 0], r2a.at[j, o - 1], on_x(o)))
        arrived(firsts[1])
        for o in reversed(range(ny)):
            to = lax.rem(y + o, ny)
            value = grad[j, to, x, 1].astype(F32)
            for n in range(nx - 1):
                value += r1b[j, n, to].astype(F32)
            if o == 0:
                out[j, half:] = value
            else:
                grad[j, to, x, 1] = value.astype(BF16)
                along_y.append(push(grad.at[j, to, x, 1], r2b.at[j, o - 1], on_y(o)))
        return along_x, along_y

    def sums_last(j, kind, seconds):
        r2a, r2b, out, half = kind[3:]
        arrived(seconds[0])
        value = out[j, :half]
        for n in range(nx - 1):
            value += r2a[j, n].astype(F32)
        out[j, :half] = value
        arrived(seconds[1])
        value = out[j, half:]
        for n in range(ny - 1):
            value += r2b[j, n].astype(F32)
        out[j, half:] = value

    for s in range(1, nz - 1):
        chain_step(s)
    arrived(second0)
    lax.fori_loop(0, nz - 2, forward_arrived, 0)
    arrived(first1)
    second1 = weights_second(1)
    forward_arrived(nz - 2, 0)
    chain_step(nz - 1)
    forward_arrived(nz - 1, 0)
    gradients_out(0)
    first_out = sums_first(0, kinds[1])
    gradients_in(0)
    firsts0 = [sums_first(0, kinds[0]), first_out]
    arrived(second1)
    lax.fori_loop(0, nz // group, forward_all, 0)
    gradients_in(1)
    firsts1 = [sums_first(1, kinds[0])]
    def dx_pair(to):
        return pltpu.make_async_remote_copy(
            src_ref=dxp.at[to, 1 - c], dst_ref=dx_r1.at[to],
            send_sem=dxp_send.at[to], recv_sem=dxp_recv.at[to],
            device_id=partner, device_id_type=pl.DeviceIdType.MESH,
        )

    def dx_spread(to, slot):
        return pltpu.make_async_remote_copy(
            src_ref=dxp.at[to, c], dst_ref=dx_r2.at[slot],
            send_sem=dxs_send.at[to], recv_sem=dxs_recv.at[slot],
            device_id=on_z(to), device_id_type=pl.DeviceIdType.MESH,
        )

    def dx_step(i, carry):
        to = lax.rem(z + 1 + i, nz)
        r = pl.ds(pl.multiple_of(to * (2 * tok), 2 * tok), 2 * tok)
        value = dot_nt(pre[0, r, :], w_in[0].reshape(width, cols_in))
        value += dot_nt(pre[1, r, :], w_in[1].reshape(width, cols_in))
        dxp[to, :, :, :width] = value.astype(BF16).reshape(2, tok, width)
        dx_pair(to).start()

        @pl.when(i > 0)
        def _():
            last = lax.rem(z + i, nz)
            dx_pair(last).wait_recv()
            dxp[last, c] = (dxp[last, c].astype(F32) + dx_r1[last].astype(F32)).astype(BF16)
            dx_spread(last, z).start()

        return carry

    lax.fori_loop(0, nz, dx_step, 0)
    seconds0 = [sums_second(0, kinds[0], firsts0[0])]
    gradients_out(1)
    firsts1.append(sums_first(1, kinds[1]))
    seconds0.append(sums_second(0, kinds[1], firsts0[1]))
    seconds1 = [sums_second(1, kind, first) for kind, first in zip(kinds, firsts1)]
    for kind, second in zip(kinds, seconds0):
        sums_last(0, kind, second)

    dx_pair(z).wait_recv()
    value = dxp[z, c].astype(F32) + dx_r1[z].astype(F32)
    for o in range(1, nz):
        source = lax.rem(z + o, nz)
        dx_spread(source, source).wait_recv()
        value += dx_r2[source].astype(F32)
    gtok_ref[...] = value[:, :width].astype(BF16)
    back = value[:, width:].T
    for k in range(top):
        ggate_ref[k : k + 1, :] = jnp.sum(
            jnp.where(ids[k : k + 1] == expert, back, 0.0), axis=0, keepdims=True
        )

    for kind, second in zip(kinds, seconds1):
        sums_last(1, kind, second)

    for copy in started:
        copy.wait_send()

    def drain(origin):
        side(origin).wait_send()
        dx_pair(origin).wait_send()

        @pl.when(origin != z)
        def _():
            dx_spread(origin, z).wait_send()

        @pl.when((origin <= z) & (z < nz - 1))
        def _():
            up(origin).wait_send()

        @pl.when((origin >= z) & (z > 0))
        def _():
            down(origin).wait_send()

    for zz in range(nz):
        drain(zz)


def emit(gtok, ggu, gd, gtok_out, ggu_out, gd_out, gtok_v, ggu_v, gd_v, sems_in, sems_out):
    parts = [(gtok, gtok_v, gtok_out)]
    for j in range(EXP_DEV):
        for src, mid, dst in ((ggu, ggu_v, ggu_out), (gd, gd_v, gd_out)):
            half = src.shape[1] // 2
            for h in range(2):
                at = pl.ds(h * half, half)
                parts.append((src.at[j, at], mid.at[j, at], dst.at[j, at]))
    ins = [pltpu.make_async_copy(s, m, sems_in.at[i]) for i, (s, m, _) in enumerate(parts)]
    outs = [pltpu.make_async_copy(m, d, sems_out.at[i]) for i, (_, m, d) in enumerate(parts)]
    for copy in ins:
        copy.start()
    for first, second in zip(ins, outs):
        first.wait()
        second.start()
    for copy in outs:
        copy.wait()


def body(ny, nx, nz, tokens, cotangent, expert_ids, gate_probs, gate_up, down_proj):
    tok, width = tokens.shape
    rows_in, cols_in = gate_up.shape[1:]
    rows_out = down_proj.shape[1]
    hi, ho = rows_in // 2, rows_out // 2
    total = nz * 2 * tok
    copies = 16 * (nx + ny - 2)
    V = pltpu.VMEM
    dma = pltpu.SemaphoreType.DMA
    e = EXP_DEV
    flops = 2 * e * total * width * cols_in * 4
    gtok, ggate, ggu, gd = pl.pallas_call(
        functools.partial(kernel, ny, nx, nz),
        out_shape=(
            jax.ShapeDtypeStruct(tokens.shape, BF16),
            jax.ShapeDtypeStruct(gate_probs.shape[::-1], F32),
            jax.ShapeDtypeStruct(gate_up.shape, F32),
            jax.ShapeDtypeStruct(down_proj.shape, F32),
        ),
        in_specs=[pl.BlockSpec(memory_space=V)] * 4 + [pl.BlockSpec(memory_space=pl.ANY)] * 2,
        out_specs=[pl.BlockSpec(memory_space=V)] * 4,
        scratch_shapes=[
            V((nz, 2, tok, 2 * width + LANES), BF16),
            V((width, total), BF16),
            V((e, ny, nx, 2, hi, cols_in), BF16),
            V((e, ny, nx, 2, ho, width), BF16),
            V((e, total, cols_in), BF16),
            V((cols_in // 2, total), BF16),
            V((e, ny, nx, 2, hi, cols_in), BF16),
            V((e, ny, nx, 2, ho, width), BF16),
            V((e, ny - 1, nx, hi, cols_in), BF16),
            V((e, nx - 1, ny, hi, cols_in), BF16),
            V((e, nx - 1, hi, cols_in), BF16),
            V((e, ny - 1, hi, cols_in), BF16),
            V((e, ny - 1, nx, ho, width), BF16),
            V((e, nx - 1, ny, ho, width), BF16),
            V((e, nx - 1, ho, width), BF16),
            V((e, ny - 1, ho, width), BF16),
            V((nz, 2, tok, width + LANES), BF16),
            V((nz, tok, width + LANES), BF16),
            V((nz, tok, width + LANES), BF16),
            dma((copies,)),
            dma((copies,)),
            dma((nz,)),
            dma((nz,)),
            dma((nz,)),
            dma((nz,)),
            dma((nz,)),
            dma((4,)),
            dma((nz,)),
            dma((nz,)),
            dma((nz,)),
            dma((nz,)),
        ],
        compiler_params=pltpu.CompilerParams(
            collective_id=0, has_side_effects=True, vmem_limit_bytes=60 * 2**20
        ),
        cost_estimate=pl.CostEstimate(flops=flops, bytes_accessed=8 * 2**20, transcendentals=0),
    )(
        tokens, cotangent, expert_ids.T, gate_probs.T,
        gate_up.reshape(e, 2, hi, cols_in), down_proj.reshape(e, 2, ho, width),
    )
    gtok, ggu, gd = pl.pallas_call(
        emit,
        out_shape=tuple(jax.ShapeDtypeStruct(a.shape, a.dtype) for a in (gtok, ggu, gd)),
        in_specs=[pl.BlockSpec(memory_space=pl.ANY)] * 3,
        out_specs=[pl.BlockSpec(memory_space=pl.ANY)] * 3,
        scratch_shapes=[V(a.shape, a.dtype) for a in (gtok, ggu, gd)] + [dma((4 * e + 1,))] * 2,
        compiler_params=pltpu.CompilerParams(vmem_limit_bytes=60 * 2**20),
    )(gtok, ggu, gd)
    return gtok, ggate.astype(BF16).T, ggu, gd


def solution(mesh):
    dp = mesh.shape["dp"]
    nx = next(n for n in range(math.isqrt(dp), 0, -1) if dp % n == 0)
    tok = P(("dp", "expert"), None)
    wgt = P("expert", "dp", None)
    return jax.shard_map(
        functools.partial(body, dp // nx, nx, mesh.shape["expert"] // 2),
        mesh=mesh,
        in_specs=(tok, tok, tok, tok, wgt, wgt),
        out_specs=(tok, tok, wgt, wgt),
        check_vma=False,
    )
```
